512 devices in a mesh: dp: 256 (over x, z, y_hi, core), feat: 2 (over y_lo).
Axes of the slice: x: 4, y: 4 (y_hi: 2, y_lo: 2; y = y_hi * 2 + y_lo), z: 16, core: 2. Of those that a mesh axis runs over, the one named last changes fastest.
Arguments:
- image_feats: bfloat16 [32768, 1536], P('dp'), may hold values from -6 to 6
- text_emb: bfloat16 [32768, 1536], P('dp', 'feat'), may hold values from -6 to 6
- image_proj: bfloat16 [1536, 1536], P(None, 'feat'), may hold values from -0.15625 to 0.15625
- log_temp: float32 [1], replicated, may hold values from 4.1 to 4.8
- bias: float32 [1], replicated, may hold values from -4 to -1
Outputs:
- image_grad: float32 [32768, 1536], P('dp', 'feat')
- text_grad: float32 [32768, 1536], P('dp', 'feat')
The draws below stay inside these ranges and needn't reach their ends.
All inputs are finite; a program needn't handle non-finite values.
Results may differ from the reference program's by a relative error of at most 0.0059.
Values may be sent and summed in bfloat16 or wider, within the bound.
A program may use at most 64 MiB of HBM per device.

```python
import jax
import jax.numpy as jnp
from jax import lax

H = 1536
E = 1536
ROWS = 128
GROUP = 16
BATCH = 32768


def steps_of(stream_key, dims, pieces, low, high):
    level, own = 1.0, jax.random.fold_in(stream_key, 6)
    for axis_at, shards_of in pieces:
        heights = jnp.exp(jax.random.uniform(jax.random.fold_in(own, axis_at), (shards_of,), jnp.float32, low / len(pieces), high / len(pieces)))
        level = level * jnp.repeat(heights, dims[axis_at] // shards_of).reshape([-1 if axis == axis_at else 1 for axis in range(len(dims))])
    return level


def centred(own_key, shape, deviation, most, cuts=(), kind=jnp.bfloat16):
    result = jax.random.normal(own_key, shape, jnp.float32) * deviation
    if len(cuts) > 0:
        result = steps_of(own_key, shape, cuts, -0.22, 0.18) * result
    return jnp.clip(result, min=-most, max=most).astype(kind)


def setup_inputs(seed: int = 0) -> dict:
    arg_keys = jax.random.split(jax.random.key(seed), 6)
    image_feats = centred(arg_keys[0], (BATCH, H), 1.0, 6.0, ((0, 256),))
    text_emb = centred(arg_keys[1], (BATCH, E), 1.0, 6.0, ((0, 256), (1, 2)))
    image_proj = centred(arg_keys[2], (H, E), H ** -0.5, 0.15625, ((1, 2),))
    log_temp = jnp.clip(jax.random.uniform(arg_keys[3], (1,), jnp.float32, 4.1, 4.8), 4.1, 4.8)
    bias = jnp.clip(jax.random.uniform(arg_keys[4], (1,), jnp.float32, -4.0, -1.0), -4.0, -1.0)
    return dict(image_feats=image_feats, text_emb=text_emb, image_proj=image_proj, log_temp=log_temp, bias=bias)


EPS = 1e-06

def unit_rows(emb):
    norm = jnp.sqrt(lax.optimization_barrier(jnp.sum(emb * emb, axis=1, keepdims=True)) + EPS)
    return (emb / norm, norm)

def reference(image_feats, text_emb, image_proj, log_temp, bias):
    img_emb = jnp.dot(image_feats, image_proj, preferred_element_type=jnp.float32)
    txt_emb = text_emb.astype(jnp.float32)
    img_unit32, img_norm = unit_rows(img_emb)
    txt_unit32, txt_norm = unit_rows(txt_emb)
    img_unit = img_unit32.astype(jnp.bfloat16)
    txt_unit = txt_unit32.astype(jnp.bfloat16)
    scale = jnp.exp(log_temp[0])
    offset = bias[0]
    group_rows = GROUP * ROWS
    groups = img_unit.shape[0] // group_rows
    width = img_unit.shape[1]

    def group_back(units):
        left, right = units
        logits = scale * jnp.dot(left, right.T, preferred_element_type=jnp.float32) + offset
        weights = (jax.nn.sigmoid(logits) - jnp.eye(group_rows, dtype=jnp.float32)).astype(jnp.bfloat16)
        first = scale * jnp.dot(weights, right, preferred_element_type=jnp.float32)
        second = scale * jnp.dot(weights.T, left, preferred_element_type=jnp.float32)
        return (first, second)
    img_back, txt_back = lax.map(group_back, (img_unit.reshape(groups, group_rows, width), txt_unit.reshape(groups, group_rows, width)))
    img_back = img_back.reshape(-1, width)
    txt_back = txt_back.reshape(-1, width)
    img_dir = ((img_back - img_unit32 * lax.optimization_barrier(jnp.sum(img_unit32 * img_back, axis=1, keepdims=True))) / img_norm).astype(jnp.bfloat16)
    text_grad = (txt_back - txt_unit32 * lax.optimization_barrier(jnp.sum(txt_unit32 * txt_back, axis=1, keepdims=True))) / txt_norm
    image_grad = jnp.dot(img_dir, image_proj.T, preferred_element_type=jnp.float32)
    return (image_grad, text_grad)
```

```python
import functools

import jax
import jax.numpy as jnp
from jax import lax
from jax.experimental import pallas as pl
from jax.experimental.pallas import tpu as pltpu
from jax.sharding import PartitionSpec as P

EPS = 1e-06
MESH = pl.DeviceIdType.MESH
F32 = jnp.float32
BF16 = jnp.bfloat16
ROWS = 128
HALF = 64
LINE = 4


def dot_nt(left, right):
    return lax.dot_general(left, right, (((1,), (1,)), ((), ())), preferred_element_type=F32)


def dot_nn(left, right):
    return jnp.dot(left, right, preferred_element_type=F32)


def as_row(column):
    n = column.shape[0]
    return jnp.transpose(jnp.broadcast_to(column, (n, 128)))[0:8, :]


def as_column(row):
    n = row.shape[1]
    return jnp.transpose(jnp.broadcast_to(row, (128, n)))[:, 0:1]


def kernel(
    feats_hbm, text_hbm, proj_hbm, temp_ref, bias_ref, igrad_ref, tgrad_ref,
    feats, text, proj, iunit32, ibuf, traw, tbuf, tacc, tsend, tleft, tright, qacc, qsend, qrecv,
    rsend, rrecv, sq_out, sq_in, dot_out, dot_in, ipart, ipart_in, tpart, tpart_in,
    lsem, swap_s, swap_r, sq_s, sq_r, ig_s, ig_r, core_s, core_r, tf_right, tf_left, tf_r,
    tb_s, tb_left, tb_right, q_s, q_r, rs_s, rs_r, dot_s, dot_r, ip_s, ip_r, tp_s, tp_r,
):
    dp = lax.axis_index("dp")
    f = lax.axis_index("feat")
    zz = (dp // 4) % 4
    h = (dp // 2) % 2
    c = dp % 2
    core = (dp + 1 - 2 * c, f)
    near_a = (dp, 1 - f)
    near_b = (dp + 2 - 4 * h, 1 - f)
    z_up = (dp + 4, f)
    z_down = (dp - 4, f)
    has_up = zz < LINE - 1
    has_down = zz > 0

    def remote(src, dst, send, recv, to):
        return pltpu.make_async_remote_copy(
            src_ref=src, dst_ref=dst, send_sem=send, recv_sem=recv, device_id=to, device_id_type=MESH
        )

    sent = []

    def send(src, dst, s, r, to):
        copy = remote(src, dst, s, r, to)
        copy.start()
        sent.append(copy)

    def arrived(dst, r):
        remote(dst, dst, q_s.at[0], r, core).wait_recv()

    loads = [
        pltpu.make_async_copy(text_hbm, text, lsem.at[0]),
        pltpu.make_async_copy(feats_hbm, feats, lsem.at[1]),
        pltpu.make_async_copy(proj_hbm, proj, lsem.at[2]),
    ]
    for load in loads:
        load.start()

    barrier = pltpu.get_barrier_semaphore()
    for peer in (core, near_a, near_b):
        pl.semaphore_signal(barrier, inc=1, device_id=peer, device_id_type=MESH)

    @pl.when(has_up)
    def _():
        pl.semaphore_signal(barrier, inc=1, device_id=z_up, device_id_type=MESH)

    @pl.when(has_down)
    def _():
        pl.semaphore_signal(barrier, inc=1, device_id=z_down, device_id_type=MESH)

    pl.semaphore_wait(barrier, 3 + has_up.astype(jnp.int32) + has_down.astype(jnp.int32))

    scale = jnp.exp(jnp.full((1, 1), temp_ref[0], F32))
    offset = bias_ref[0]

    loads[0].wait()
    theirs = pl.multiple_of(HALF * (1 - f), HALF)
    mine = pl.multiple_of(HALF * f, HALF)
    send(text.at[pl.ds(theirs, HALF)], traw.at[f], swap_s.at[0], swap_r.at[0], near_a)
    traw[f] = text[pl.ds(mine, HALF), :]

    loads[1].wait()
    loads[2].wait()
    emb = dot_nn(feats[...], proj[...])
    iunit32[...] = emb
    sq_out[...] = as_row(jnp.sum(emb * emb, axis=1, keepdims=True))
    send(sq_out, sq_in, sq_s.at[0], sq_r.at[0], near_a)

    arrived(traw.at[1 - f], swap_r.at[0])
    t0 = traw[0].astype(F32)
    t1 = traw[1].astype(F32)
    tnorm = jnp.sqrt(jnp.sum(t0 * t0 + t1 * t1, axis=1, keepdims=True) + EPS)
    own_t = pl.ds(pl.multiple_of(zz * HALF, HALF), HALF)
    tbuf[0, own_t] = (t0 / tnorm).astype(BF16)
    tbuf[1, own_t] = (t1 / tnorm).astype(BF16)

    line_copies = []

    def block(ref, e, b):
        return ref.at[e, pl.ds(pl.multiple_of(b * HALF, HALF), HALF)]

    def t_forward(dist):
        for sign, can, to, sems in ((-1, has_up, z_up, tf_right), (1, has_down, z_down, tf_left)):
            b = zz + sign * dist
            here = (b >= 0) if sign < 0 else (b < LINE)

            @pl.when(here)
            def _():
                for e in range(2):
                    if dist > 0:
                        arrived(block(tbuf, e, b), tf_r.at[b, e])

                    @pl.when(can)
                    def _():
                        remote(block(tbuf, e, b), block(tbuf, e, b), sems.at[dist, e], tf_r.at[b, e], to).start()

    def t_forward_sent(dist):
        for sign, can, to, sems in ((-1, has_up, z_up, tf_right), (1, has_down, z_down, tf_left)):
            b = zz + sign * dist
            here = (b >= 0) if sign < 0 else (b < LINE)

            @pl.when(jnp.logical_and(here, can))
            def _():
                for e in range(2):
                    remote(block(tbuf, e, b), block(tbuf, e, b), sems.at[dist, e], tf_r.at[b, e], to).wait_send()

    t_forward(0)

    arrived(sq_in, sq_r.at[0])
    inorm = jnp.sqrt(as_column(sq_out[0:1, :] + sq_in[0:1, :]) + EPS)
    unit32 = iunit32[...] / inorm
    iunit32[...] = unit32

    def img(width, core_at, high, part=None):
        start = (core_at * 2 + high) * ROWS + (0 if part is None else part * HALF)
        size = ROWS if part is None else HALF
        return ibuf.at[width, pl.ds(pl.multiple_of(start, HALF), size)]

    ibuf[f, pl.ds(pl.multiple_of((c * 2 + h) * ROWS, ROWS), ROWS)] = unit32.astype(BF16)

    def give(part_ref, slot, to):
        send(part_ref, part_ref, ig_s.at[slot], ig_r.at[slot], to)

    give(img(f, c, h, 0), 0, near_a)
    give(img(f, c, h, 1), 3, near_b)
    give(img(f, c, h, 1), 1, near_a)
    give(img(f, c, h, 0), 2, near_b)

    def share(piece, slot):
        send(piece, piece, core_s.at[slot], core_r.at[slot], core)

    share(img(f, c, h), 0)
    t_forward(1)
    arrived(img(1 - f, c, h, 0), ig_r.at[0])
    give(img(1 - f, c, h, 0), 4, near_b)
    arrived(img(1 - f, c, 1 - h, 1), ig_r.at[3])
    give(img(1 - f, c, 1 - h, 1), 5, near_a)
    arrived(img(1 - f, c, h, 1), ig_r.at[1])
    share(img(1 - f, c, h), 1)
    arrived(img(1 - f, c, 1 - h, 0), ig_r.at[2])
    share(img(1 - f, c, 1 - h), 2)
    t_forward(2)
    arrived(img(f, c, 1 - h, 0), ig_r.at[4])
    arrived(img(f, c, 1 - h, 1), ig_r.at[5])
    share(img(f, c, 1 - h), 3)
    t_forward(3)
    arrived(img(f, 1 - c, h), core_r.at[0])
    arrived(img(1 - f, 1 - c, h), core_r.at[1])
    arrived(img(1 - f, 1 - c, 1 - h), core_r.at[2])
    arrived(img(f, 1 - c, 1 - h), core_r.at[3])

    sums = dot_nt(ibuf[0], tbuf[0]) + dot_nt(ibuf[1], tbuf[1])
    logits = scale * sums + offset
    row = lax.broadcasted_iota(jnp.int32, logits.shape, 0) - ((c * 2 + h) * ROWS + mine)
    col = lax.broadcasted_iota(jnp.int32, logits.shape, 1) - zz * HALF
    same = jnp.logical_and(row == col, jnp.logical_and(col >= 0, col < HALF))
    weights32 = jax.nn.sigmoid(logits) - jnp.where(same, 1.0, 0.0)
    weights = weights32.astype(BF16)
    weights_t = jnp.transpose(weights32).astype(BF16)

    for e in range(2):
        tacc[e] = scale * dot_nn(weights_t, ibuf[e])

    def t_back(dist):
        for sign, can, to, inbox, r, there in (
            (-1, has_up, z_down, tright, tb_right, has_down),
            (1, has_down, z_up, tleft, tb_left, has_up),
        ):
            b = zz + sign * dist
            here = (b >= 0) if sign < 0 else (b < LINE)

            @pl.when(here)
            def _():
                at = pl.ds(pl.multiple_of(b * HALF, HALF), HALF)
                for e in range(2):

                    @pl.when(can)
                    def _():
                        arrived(inbox.at[e, at], r.at[b, e])
                        tsend[e, at] = (tacc[e, at] + inbox[e, at].astype(F32)).astype(BF16)

                    @pl.when(jnp.logical_not(can))
                    def _():
                        tsend[e, at] = tacc[e, at].astype(BF16)

                    remote(tsend.at[e, at], inbox.at[e, at], tb_s.at[b, e], r.at[b, e], to).start()

    def t_back_sent(dist):
        for sign, to, inbox, r in ((-1, z_down, tright, tb_right), (1, z_up, tleft, tb_left)):
            b = zz + sign * dist
            here = (b >= 0) if sign < 0 else (b < LINE)

            @pl.when(here)
            def _():
                at = pl.ds(pl.multiple_of(b * HALF, HALF), HALF)
                for e in range(2):
                    remote(tsend.at[e, at], inbox.at[e, at], tb_s.at[b, e], r.at[b, e], to).wait_send()

    t_back(3)

    other = pl.ds(pl.multiple_of((1 - c) * 2 * ROWS, ROWS), 2 * ROWS)
    own = pl.ds(pl.multiple_of(c * 2 * ROWS, ROWS), 2 * ROWS)
    for e in range(2):
        qacc[e] = scale * dot_nn(weights, tbuf[e])
        qsend[e] = qacc[e, other].astype(BF16)
        send(qsend.at[e], qrecv.at[e], q_s.at[e], q_r.at[e], core)

    t_back(2)

    def quarter(width, high, part):
        start = (c * 2 + high) * ROWS + part * HALF
        return width, pl.ds(pl.multiple_of(start, HALF), HALF)

    for e in range(2):
        arrived(qrecv.at[e], q_r.at[e])
        qacc[e, own] = qacc[e, own] + qrecv[e].astype(F32)

    def hand(slot, value, to):
        rsend[slot] = value.astype(BF16)
        send(rsend.at[slot], rrecv.at[slot], rs_s.at[slot], rs_r.at[slot], to)

    def got(slot):
        arrived(rrecv.at[slot], rs_r.at[slot])
        return rrecv[slot].astype(F32)

    hand(0, qacc[quarter(f, 1 - h, 0)], near_a)
    hand(1, qacc[quarter(f, 1 - h, 1)], near_b)
    hand(2, qacc[quarter(1 - f, h, 0)], near_a)
    hand(5, qacc[quarter(1 - f, 1 - h, 1)], near_b)
    t_back(1)
    hand(4, qacc[quarter(1 - f, 1 - h, 0)] + got(0), near_b)
    hand(3, qacc[quarter(1 - f, h, 1)] + got(1), near_a)

    for e in range(2):

        @pl.when(has_down)
        def _():
            arrived(block(tleft, e, zz), tb_left.at[zz, e])
            tacc[e, own_t] = tacc[e, own_t] + tleft[e, own_t].astype(F32)

        @pl.when(has_up)
        def _():
            arrived(block(tright, e, zz), tb_right.at[zz, e])
            tacc[e, own_t] = tacc[e, own_t] + tright[e, own_t].astype(F32)

    u0 = traw[0].astype(F32) / tnorm
    u1 = traw[1].astype(F32) / tnorm
    b0 = tacc[0, own_t]
    b1 = tacc[1, own_t]
    tdot = jnp.sum(u0 * b0 + u1 * b1, axis=1, keepdims=True)
    tacc[0, own_t] = (b0 - u0 * tdot) / tnorm
    tacc[1, own_t] = (b1 - u1 * tdot) / tnorm
    tpart[...] = tacc[1 - f, own_t].astype(BF16)
    send(tpart, tpart_in, tp_s.at[0], tp_r.at[0], near_a)
    tgrad_ref[pl.ds(mine, HALF), :] = tacc[f, own_t]

    low = qacc[quarter(f, h, 0)] + got(2) + got(4)
    high = qacc[quarter(f, h, 1)] + got(3) + got(5)
    back = jnp.concatenate([low, high], axis=0)
    unit = iunit32[...]
    dot_out[...] = as_row(jnp.sum(unit * back, axis=1, keepdims=True))
    send(dot_out, dot_in, dot_s.at[0], dot_r.at[0], near_a)
    arrived(dot_in, dot_r.at[0])
    idot = as_column(dot_out[0:1, :] + dot_in[0:1, :])
    direction = ((back - unit * idot) / inorm).astype(BF16)
    width = proj.shape[1]
    theirs_h = pl.ds(pl.multiple_of((1 - f) * width, width), width)
    mine_h = pl.ds(pl.multiple_of(f * width, width), width)
    ipart[...] = dot_nt(direction, proj[theirs_h, :]).astype(BF16)
    send(ipart, ipart_in, ip_s.at[0], ip_r.at[0], near_a)
    ours = dot_nt(direction, proj[mine_h, :])

    arrived(tpart_in, tp_r.at[0])
    tgrad_ref[pl.ds(theirs, HALF), :] = tpart_in[...].astype(F32)
    arrived(ipart_in, ip_r.at[0])
    igrad_ref[...] = ours + ipart_in[...].astype(F32)

    for copy in sent:
        copy.wait_send()
    for dist in range(LINE):
        t_forward_sent(dist)
        if dist > 0:
            t_back_sent(dist)


def local(image_feats, text_emb, image_proj, log_temp, bias):
    rows, wide = image_feats.shape
    width = text_emb.shape[1]
    dma = pltpu.SemaphoreType.DMA
    group = 4 * rows
    text_rows = LINE * HALF
    return pl.pallas_call(
        kernel,
        out_shape=(jax.ShapeDtypeStruct((rows, width), F32), jax.ShapeDtypeStruct((rows, width), F32)),
        in_specs=[pl.BlockSpec(memory_space=pl.ANY)] * 3 + [pl.BlockSpec(memory_space=pltpu.SMEM)] * 2,
        out_specs=(pl.BlockSpec(memory_space=pltpu.VMEM), pl.BlockSpec(memory_space=pltpu.VMEM)),
        scratch_shapes=[
            pltpu.VMEM((rows, wide), BF16),
            pltpu.VMEM((rows, width), BF16),
            pltpu.VMEM((wide, width), BF16),
            pltpu.VMEM((rows, width), F32),
            pltpu.VMEM((2, group, width), BF16),
            pltpu.VMEM((2, HALF, width), BF16),
            pltpu.VMEM((2, text_rows, width), BF16),
            pltpu.VMEM((2, text_rows, width), F32),
            pltpu.VMEM((2, text_rows, width), BF16),
            pltpu.VMEM((2, text_rows, width), BF16),
            pltpu.VMEM((2, text_rows, width), BF16),
            pltpu.VMEM((2, group, width), F32),
            pltpu.VMEM((2, 2 * rows, width), BF16),
            pltpu.VMEM((2, 2 * rows, width), BF16),
            pltpu.VMEM((6, HALF, width), BF16),
            pltpu.VMEM((6, HALF, width), BF16),
            pltpu.VMEM((8, rows), F32),
            pltpu.VMEM((8, rows), F32),
            pltpu.VMEM((8, rows), F32),
            pltpu.VMEM((8, rows), F32),
            pltpu.VMEM((rows, width), BF16),
            pltpu.VMEM((rows, width), BF16),
            pltpu.VMEM((HALF, width), BF16),
            pltpu.VMEM((HALF, width), BF16),
            dma((3,)),
            dma((1,)), dma((1,)),
            dma((1,)), dma((1,)),
            dma((6,)), dma((6,)),
            dma((4,)), dma((4,)),
            dma((4, 2)), dma((4, 2)), dma((4, 2)),
            dma((4, 2)), dma((4, 2)), dma((4, 2)),
            dma((2,)), dma((2,)),
            dma((6,)), dma((6,)),
            dma((1,)), dma((1,)),
            dma((1,)), dma((1,)),
            dma((1,)), dma((1,)),
        ],
        compiler_params=pltpu.CompilerParams(
            collective_id=0, has_side_effects=True, vmem_limit_bytes=48 << 20
        ),
        name="contrastive_backward",
    )(image_feats, text_emb, image_proj, log_temp, bias)


def solution(mesh):
    placed = (P("dp", None), P("dp", "feat"), P(None, "feat"), P(), P())
    return jax.shard_map(
        local,
        mesh=mesh,
        in_specs=placed,
        out_specs=(P("dp", "feat"), P("dp", "feat")),
        check_vma=False,
    )
```

```python
import functools

import jax
import jax.numpy as jnp
from jax import lax
from jax.experimental import pallas as pl
from jax.experimental.pallas import tpu as pltpu
from jax.sharding import PartitionSpec as P

EPS = 1e-06
MESH = pl.DeviceIdType.MESH
F32 = jnp.float32
BF16 = jnp.bfloat16
ROWS = 128
HALF = 64
LINE = 4


def dot_nt(left, right):
    return lax.dot_general(left, right, (((1,), (1,)), ((), ())), preferred_element_type=F32)


def dot_nn(left, right):
    return jnp.dot(left, right, preferred_element_type=F32)


def as_row(column):
    n = column.shape[0]
    return jnp.transpose(jnp.broadcast_to(column, (n, 128)))[0:8, :]


def as_column(row):
    n = row.shape[1]
    return jnp.transpose(jnp.broadcast_to(row, (128, n)))[:, 0:1]


def kernel(
    feats_hbm, text_hbm, proj_hbm, temp_ref, bias_ref, igrad_ref, tgrad_ref,
    feats, text, proj, iunit32, ibuf, tbuf, tunit, tnorms, tacc, tsend, tleft, tright, qacc, qsend, qrecv,
    rsend, rrecv, sq_out, sq_in, dots, dot_all, dot_core, dot_out, dot_in, ipart, ipart_in, tpart, tpart_in,
    lsem, sq_s, sq_r, ig_s, ig_r, core_s, core_r, tf_swap, tf_up, tf_down, tf_r,
    tb_s, tb_left, tb_right, q_s, q_r, rs_s, rs_r, dc_s, dc_r, dot_s, dot_r, ip_s, ip_r, tp_s, tp_r,
):
    dp = lax.axis_index("dp")
    f = lax.axis_index("feat")
    zz = (dp // 4) % 4
    h = (dp // 2) % 2
    c = dp % 2
    opposite = dp + 2 - 4 * h
    core = (dp + 1 - 2 * c, f)
    near_a = (dp, 1 - f)
    near_b = (opposite, 1 - f)
    far = (opposite, f)
    z_up = (dp + 4, f)
    z_down = (dp - 4, f)
    has_up = zz < LINE - 1
    has_down = zz > 0

    def remote(src, dst, send, recv, to):
        return pltpu.make_async_remote_copy(
            src_ref=src, dst_ref=dst, send_sem=send, recv_sem=recv, device_id=to, device_id_type=MESH
        )

    sent = []

    def send(src, dst, s, r, to):
        copy = remote(src, dst, s, r, to)
        copy.start()
        sent.append(copy)

    def arrived(dst, r):
        remote(dst, dst, q_s.at[0], r, core).wait_recv()

    loads = [
        pltpu.make_async_copy(text_hbm, text, lsem.at[0]),
        pltpu.make_async_copy(feats_hbm, feats, lsem.at[1]),
        pltpu.make_async_copy(proj_hbm, proj, lsem.at[2]),
    ]
    for load in loads:
        load.start()

    barrier = pltpu.get_barrier_semaphore()
    for peer in (core, near_a, near_b, far):
        pl.semaphore_signal(barrier, inc=1, device_id=peer, device_id_type=MESH)

    @pl.when(has_up)
    def _():
        pl.semaphore_signal(barrier, inc=1, device_id=z_up, device_id_type=MESH)

    @pl.when(has_down)
    def _():
        pl.semaphore_signal(barrier, inc=1, device_id=z_down, device_id_type=MESH)

    loads[0].wait()
    pl.semaphore_wait(barrier, 4 + has_up.astype(jnp.int32) + has_down.astype(jnp.int32))

    scale = jnp.exp(jnp.full((1, 1), temp_ref[0], F32))
    offset = bias_ref[0]

    theirs = pl.ds(pl.multiple_of(HALF * (1 - f), HALF), HALF)
    mine = pl.ds(pl.multiple_of(HALF * f, HALF), HALF)

    def rows_of(b):
        return pl.ds(pl.multiple_of(b * HALF, HALF), HALF)

    def block(ref, e, b):
        return ref.at[e, rows_of(b)]

    own_t = rows_of(zz)
    send(text.at[theirs], block(tbuf, f, zz), tf_swap.at[0], tf_r.at[zz, f], near_a)

    def t_forward(dist, e, src=None):
        for sign, can, to, sems in ((-1, has_up, z_up, tf_up), (1, has_down, z_down, tf_down)):
            b = zz + sign * dist
            here = (b >= 0) if sign < 0 else (b < LINE)

            @pl.when(here)
            def _():
                if dist > 0:
                    arrived(block(tbuf, e, b), tf_r.at[b, e])

                @pl.when(can)
                def _():
                    origin = block(tbuf, e, b) if src is None else src
                    remote(origin, block(tbuf, e, b), sems.at[dist, e], tf_r.at[b, e], to).start()

    def t_forward_sent(dist, e):
        for sign, can, to, sems in ((-1, has_up, z_up, tf_up), (1, has_down, z_down, tf_down)):
            b = zz + sign * dist
            here = (b >= 0) if sign < 0 else (b < LINE)

            @pl.when(jnp.logical_and(here, can))
            def _():
                remote(block(tbuf, e, b), block(tbuf, e, b), sems.at[dist, e], tf_r.at[b, e], to).wait_send()

    def normalise(b):
        at = rows_of(b)
        t0 = tbuf[0, at].astype(F32)
        t1 = tbuf[1, at].astype(F32)
        norm = jnp.sqrt(jnp.sum(t0 * t0 + t1 * t1, axis=1, keepdims=True) + EPS)
        tnorms[at] = jnp.broadcast_to(norm, (HALF, 128))
        tunit[0, at] = (t0 / norm).astype(BF16)
        tunit[1, at] = (t1 / norm).astype(BF16)

    def normalise_at(dist):
        for b, here in ((zz - dist, zz - dist >= 0), (zz + dist, zz + dist < LINE)):

            @pl.when(here)
            def _():
                normalise(b)

    t_forward(0, f, text.at[mine])
    tbuf[f, own_t] = text[mine, :]

    loads[1].wait()
    loads[2].wait()
    emb = dot_nn(feats[...], proj[...])
    iunit32[...] = emb
    sq_out[...] = as_row(jnp.sum(emb * emb, axis=1, keepdims=True))
    send(sq_out, sq_in, sq_s.at[0], sq_r.at[0], near_a)

    arrived(block(tbuf, 1 - f, zz), tf_r.at[zz, 1 - f])
    t_forward(0, 1 - f)
    normalise(zz)

    arrived(sq_in, sq_r.at[0])
    inorm = jnp.sqrt(as_column(sq_out[0:1, :] + sq_in[0:1, :]) + EPS)
    unit32 = iunit32[...] / inorm
    iunit32[...] = unit32

    def img(width, core_at, high, part=None):
        start = (core_at * 2 + high) * ROWS + (0 if part is None else part * HALF)
        size = ROWS if part is None else HALF
        return ibuf.at[width, pl.ds(pl.multiple_of(start, HALF), size)]

    ibuf[f, pl.ds(pl.multiple_of((c * 2 + h) * ROWS, ROWS), ROWS)] = unit32.astype(BF16)

    def give(part_ref, slot, to):
        send(part_ref, part_ref, ig_s.at[slot], ig_r.at[slot], to)

    give(img(f, c, h, 0), 0, near_a)
    give(img(f, c, h, 1), 3, near_b)
    give(img(f, c, h, 1), 1, near_a)
    give(img(f, c, h, 0), 2, near_b)

    def share(piece, slot):
        send(piece, piece, core_s.at[slot], core_r.at[slot], core)

    share(img(f, c, h), 0)
    t_forward(1, f)
    t_forward(1, 1 - f)
    arrived(img(1 - f, c, h, 0), ig_r.at[0])
    give(img(1 - f, c, h, 0), 4, near_b)
    arrived(img(1 - f, c, 1 - h, 1), ig_r.at[3])
    give(img(1 - f, c, 1 - h, 1), 5, near_a)
    normalise_at(1)
    arrived(img(1 - f, c, h, 1), ig_r.at[1])
    share(img(1 - f, c, h), 1)
    arrived(img(1 - f, c, 1 - h, 0), ig_r.at[2])
    share(img(1 - f, c, 1 - h), 2)
    t_forward(2, f)
    t_forward(2, 1 - f)
    normalise_at(2)
    arrived(img(f, c, 1 - h, 0), ig_r.at[4])
    arrived(img(f, c, 1 - h, 1), ig_r.at[5])
    share(img(f, c, 1 - h), 3)
    t_forward(3, f)
    t_forward(3, 1 - f)
    normalise_at(3)
    arrived(img(f, 1 - c, h), core_r.at[0])
    arrived(img(1 - f, 1 - c, h), core_r.at[1])
    arrived(img(1 - f, 1 - c, 1 - h), core_r.at[2])
    arrived(img(f, 1 - c, 1 - h), core_r.at[3])

    sums = dot_nt(ibuf[0], tunit[0]) + dot_nt(ibuf[1], tunit[1])
    logits = scale * sums + offset
    row = lax.broadcasted_iota(jnp.int32, logits.shape, 0) - ((c * 2 + h) * ROWS + HALF * f)
    col = lax.broadcasted_iota(jnp.int32, logits.shape, 1) - zz * HALF
    same = jnp.logical_and(row == col, jnp.logical_and(col >= 0, col < HALF))
    weights32 = jax.nn.sigmoid(logits) - jnp.where(same, 1.0, 0.0)
    weights = weights32.astype(BF16)
    weights_t = jnp.transpose(weights32).astype(BF16)

    for e in range(2):
        tacc[e] = dot_nn(weights_t, ibuf[e])

    def t_back(dist):
        for e in range(2):
            for sign, can, to, inbox, r in (
                (-1, has_up, z_down, tright, tb_right),
                (1, has_down, z_up, tleft, tb_left),
            ):
                b = zz + sign * dist
                here = (b >= 0) if sign < 0 else (b < LINE)

                @pl.when(here)
                def _():
                    at = rows_of(b)

                    @pl.when(can)
                    def _():
                        arrived(inbox.at[e, at], r.at[b, e])
                        tsend[e, at] = (tacc[e, at] + inbox[e, at].astype(F32)).astype(BF16)

                    @pl.when(jnp.logical_not(can))
                    def _():
                        tsend[e, at] = tacc[e, at].astype(BF16)

                    remote(tsend.at[e, at], inbox.at[e, at], tb_s.at[b, e], r.at[b, e], to).start()

    def t_back_sent(dist):
        for sign, to, inbox, r in ((-1, z_down, tright, tb_right), (1, z_up, tleft, tb_left)):
            b = zz + sign * dist
            here = (b >= 0) if sign < 0 else (b < LINE)

            @pl.when(here)
            def _():
                at = rows_of(b)
                for e in range(2):
                    remote(tsend.at[e, at], inbox.at[e, at], tb_s.at[b, e], r.at[b, e], to).wait_send()

    t_back(3)

    def quarter(core_at, high, part=None):
        start = (core_at * 2 + high) * ROWS + (0 if part is None else part * HALF)
        return pl.ds(pl.multiple_of(start, HALF), ROWS if part is None else HALF)

    rows_other = pl.ds(pl.multiple_of((1 - c) * 2 * ROWS, ROWS), 2 * ROWS)
    rows_own = pl.ds(pl.multiple_of(c * 2 * ROWS, ROWS), 2 * ROWS)
    wide_weights = dots
    wide_weights[...] = weights
    order = ((f, 1 - h), (1 - f, 1 - h), (1 - f, h), (f, h))
    for slot, (width, high) in enumerate(order):
        qsend[slot] = dot_nn(wide_weights[quarter(1 - c, high), :], tunit[width]).astype(BF16)
        send(qsend.at[slot], qrecv.at[slot], q_s.at[slot], q_r.at[slot], core)

    part = jnp.sum(weights32 * sums, axis=1, keepdims=True)
    dot_all[...] = as_row(part)
    ds_other = pl.ds(pl.multiple_of((1 - c) * 2 * ROWS, ROWS), 2 * ROWS)
    ds_own = pl.ds(pl.multiple_of(c * 2 * ROWS, ROWS), 2 * ROWS)
    dot_core[0] = dot_all[:, ds_other]
    send(dot_core.at[0], dot_core.at[1], dc_s.at[0], dc_r.at[0], core)

    for e in range(2):
        qacc[e] = dot_nn(wide_weights[rows_own, :], tunit[e])

    def mid(high, part):
        return pl.ds(pl.multiple_of(high * ROWS + part * HALF, HALF), HALF)

    def whole(slot, width, high):
        arrived(qrecv.at[slot], q_r.at[slot])
        at = pl.ds(pl.multiple_of(high * ROWS, ROWS), ROWS)
        qacc[width, at] = qacc[width, at] + qrecv[slot].astype(F32)

    def hand(slot, value, to):
        rsend[slot] = value.astype(BF16)
        send(rsend.at[slot], rrecv.at[slot], rs_s.at[slot], rs_r.at[slot], to)

    def got(slot):
        arrived(rrecv.at[slot], rs_r.at[slot])
        return rrecv[slot].astype(F32)

    whole(0, f, 1 - h)
    hand(0, qacc[f, mid(1 - h, 0)], near_a)
    hand(1, qacc[f, mid(1 - h, 1)], near_b)
    whole(1, 1 - f, 1 - h)
    hand(5, qacc[1 - f, mid(1 - h, 1)], near_b)
    whole(2, 1 - f, h)
    hand(2, qacc[1 - f, mid(h, 0)], near_a)
    arrived(dot_core.at[1], dc_r.at[0])
    dot_core[2] = dot_all[:, ds_own] + dot_core[1]
    for slot, high, to in ((0, h, near_a), (1, 1 - h, near_b), (2, 1 - h, far)):
        dot_out[slot] = dot_core[2, :, pl.ds(pl.multiple_of(high * ROWS, ROWS), ROWS)]
        send(dot_out.at[slot], dot_in.at[slot], dot_s.at[slot], dot_r.at[slot], to)
    whole(3, f, h)
    t_back(2)
    hand(4, qacc[1 - f, mid(1 - h, 0)] + got(0), near_b)
    hand(3, qacc[1 - f, mid(h, 1)] + got(1), near_a)
    t_back(1)

    for slot in range(3):
        arrived(dot_in.at[slot], dot_r.at[slot])
    idot_row = dot_core[2, 0:1, pl.ds(pl.multiple_of(h * ROWS, ROWS), ROWS)]
    idot = as_column(idot_row + dot_in[0, 0:1, :] + dot_in[1, 0:1, :] + dot_in[2, 0:1, :])
    low = qacc[f, mid(h, 0)] + got(2) + got(4)
    high = qacc[f, mid(h, 1)] + got(5) + got(3)
    back = jnp.concatenate([low, high], axis=0)
    direction = ((back - iunit32[...] * idot) * (scale / inorm)).astype(BF16)
    width = proj.shape[1]
    theirs_h = pl.ds(pl.multiple_of((1 - f) * width, width), width)
    mine_h = pl.ds(pl.multiple_of(f * width, width), width)
    ipart[...] = dot_nt(direction, proj[theirs_h, :]).astype(BF16)
    send(ipart, ipart_in, ip_s.at[0], ip_r.at[0], near_a)
    igrad_ref[...] = dot_nt(direction, proj[mine_h, :])

    for e in range(2):

        @pl.when(has_down)
        def _():
            arrived(block(tleft, e, zz), tb_left.at[zz, e])
            tacc[e, own_t] = tacc[e, own_t] + tleft[e, own_t].astype(F32)

        @pl.when(has_up)
        def _():
            arrived(block(tright, e, zz), tb_right.at[zz, e])
            tacc[e, own_t] = tacc[e, own_t] + tright[e, own_t].astype(F32)

    tnorm = tnorms[own_t][:, 0:1]
    u0 = tbuf[0, own_t].astype(F32) / tnorm
    u1 = tbuf[1, own_t].astype(F32) / tnorm
    b0 = tacc[0, own_t]
    b1 = tacc[1, own_t]
    tdot = jnp.sum(u0 * b0 + u1 * b1, axis=1, keepdims=True)
    factor = scale / tnorm
    tacc[0, own_t] = (b0 - u0 * tdot) * factor
    tacc[1, own_t] = (b1 - u1 * tdot) * factor
    tpart[...] = tacc[1 - f, own_t].astype(BF16)
    send(tpart, tpart_in, tp_s.at[0], tp_r.at[0], near_a)
    tgrad_ref[mine, :] = tacc[f, own_t]

    arrived(ipart_in, ip_r.at[0])
    igrad_ref[...] = igrad_ref[...] + ipart_in[...].astype(F32)
    arrived(tpart_in, tp_r.at[0])
    tgrad_ref[theirs, :] = tpart_in[...].astype(F32)

    for copy in sent:
        copy.wait_send()
    for dist in range(LINE):
        for e in range(2):
            t_forward_sent(dist, e)
        if dist > 0:
            t_back_sent(dist)


def local(image_feats, text_emb, image_proj, log_temp, bias):
    rows, wide = image_feats.shape
    width = text_emb.shape[1]
    dma = pltpu.SemaphoreType.DMA
    group = 4 * rows
    text_rows = LINE * HALF
    return pl.pallas_call(
        kernel,
        out_shape=(jax.ShapeDtypeStruct((rows, width), F32), jax.ShapeDtypeStruct((rows, width), F32)),
        in_specs=[pl.BlockSpec(memory_space=pltpu.HBM)] * 3 + [pl.BlockSpec(memory_space=pltpu.SMEM)] * 2,
        out_specs=(pl.BlockSpec(memory_space=pltpu.VMEM), pl.BlockSpec(memory_space=pltpu.VMEM)),
        scratch_shapes=[
            pltpu.VMEM((rows, wide), BF16),
            pltpu.VMEM((rows, width), BF16),
            pltpu.VMEM((wide, width), BF16),
            pltpu.VMEM((rows, width), F32),
            pltpu.VMEM((2, group, width), BF16),
            pltpu.VMEM((2, text_rows, width), BF16),
            pltpu.VMEM((2, text_rows, width), BF16),
            pltpu.VMEM((text_rows, 128), F32),
            pltpu.VMEM((2, text_rows, width), F32),
            pltpu.VMEM((2, text_rows, width), BF16),
            pltpu.VMEM((2, text_rows, width), BF16),
            pltpu.VMEM((2, text_rows, width), BF16),
            pltpu.VMEM((2, 2 * rows, width), F32),
            pltpu.VMEM((4, rows, width), BF16),
            pltpu.VMEM((4, rows, width), BF16),
            pltpu.VMEM((6, HALF, width), BF16),
            pltpu.VMEM((6, HALF, width), BF16),
            pltpu.VMEM((8, rows), F32),
            pltpu.VMEM((8, rows), F32),
            pltpu.VMEM((group, text_rows), BF16),
            pltpu.VMEM((8, group), F32),
            pltpu.VMEM((3, 8, 2 * rows), F32),
            pltpu.VMEM((3, 8, rows), F32),
            pltpu.VMEM((3, 8, rows), F32),
            pltpu.VMEM((rows, width), BF16),
            pltpu.VMEM((rows, width), BF16),
            pltpu.VMEM((HALF, width), BF16),
            pltpu.VMEM((HALF, width), BF16),
            dma((3,)),
            dma((1,)), dma((1,)),
            dma((6,)), dma((6,)),
            dma((4,)), dma((4,)),
            dma((1,)), dma((4, 2)), dma((4, 2)), dma((4, 2)),
            dma((4, 2)), dma((4, 2)), dma((4, 2)),
            dma((4,)), dma((4,)),
            dma((6,)), dma((6,)),
            dma((1,)), dma((1,)),
            dma((3,)), dma((3,)),
            dma((1,)), dma((1,)),
            dma((1,)), dma((1,)),
        ],
        compiler_params=pltpu.CompilerParams(
            collective_id=0, has_side_effects=True, vmem_limit_bytes=60 << 20
        ),
        name="contrastive_backward",
    )(image_feats, text_emb, image_proj, log_temp, bias)


def solution(mesh):
    placed = (P("dp", None), P("dp", "feat"), P(None, "feat"), P(), P())
    return jax.shard_map(
        local,
        mesh=mesh,
        in_specs=placed,
        out_specs=(P("dp", "feat"), P("dp", "feat")),
        check_vma=False,
    )
```

```python
import functools

import jax
import jax.numpy as jnp
from jax import lax
from jax.experimental import pallas as pl
from jax.experimental.pallas import tpu as pltpu
from jax.sharding import PartitionSpec as P

EPS = 1e-06
MESH = pl.DeviceIdType.MESH
F32 = jnp.float32
BF16 = jnp.bfloat16
ROWS = 128
HALF = 64
LINE = 4
CUTS = 4


def dot_nt(left, right):
    return lax.dot_general(left, right, (((1,), (1,)), ((), ())), preferred_element_type=F32)


def dot_nn(left, right):
    return jnp.dot(left, right, preferred_element_type=F32)


def as_row(column):
    n = column.shape[0]
    return jnp.transpose(jnp.broadcast_to(column, (n, 128)))[0:8, :]


def as_column(row):
    n = row.shape[1]
    return jnp.transpose(jnp.broadcast_to(row, (128, n)))[:, 0:1]


def kernel(
    feats_hbm, text_hbm, proj_hbm, temp_ref, bias_ref, igrad_ref, tgrad_ref,
    feats, text, proj, emb_ref, ibuf, inorms, tbuf, tunit, tnorms, weigh, wimg, tacc, tsend, tleft, tright,
    qown, qa, qb, rsend, rrecv, dot_out, dot_in, ipart, ipart_in, tpart, tpart_in,
    lsem, ig_s, ig_r, core_s, core_r, tf_swap, tf_up, tf_down, tf_r, ts_s, ts_r,
    tb_s, tb_left, tb_right, rs_s, rs_r, dot_s, dot_r, ip_s, ip_r, tp_s, tp_r,
):
    dp = lax.axis_index("dp")
    f = lax.axis_index("feat")
    zz = (dp // 4) % 4
    h = (dp // 2) % 2
    c = dp % 2
    opposite = dp + 2 - 4 * h
    core = (dp + 1 - 2 * c, f)
    near_a = (dp, 1 - f)
    near_b = (opposite, 1 - f)
    far = (opposite, f)
    z_up = (dp + 4, f)
    z_down = (dp - 4, f)
    has_up = zz < LINE - 1
    has_down = zz > 0

    def remote(src, dst, send, recv, to):
        return pltpu.make_async_remote_copy(
            src_ref=src, dst_ref=dst, send_sem=send, recv_sem=recv, device_id=to, device_id_type=MESH
        )

    sent = []

    def send(src, dst, s, r, to):
        copy = remote(src, dst, s, r, to)
        copy.start()
        sent.append(copy)

    def arrived(dst, r):
        remote(dst, dst, tf_swap.at[0], r, core).wait_recv()

    depth = proj.shape[0] // CUTS
    loads = [pltpu.make_async_copy(text_hbm, text, lsem.at[0]), pltpu.make_async_copy(feats_hbm, feats, lsem.at[1])]
    for cut in range(CUTS):
        rows = pl.ds(cut * depth, depth)
        loads.append(pltpu.make_async_copy(proj_hbm.at[rows], proj.at[rows], lsem.at[2 + cut]))
    for load in loads:
        load.start()

    barrier = pltpu.get_barrier_semaphore()
    for peer in (core, near_a, near_b, far):
        pl.semaphore_signal(barrier, inc=1, device_id=peer, device_id_type=MESH)

    @pl.when(has_up)
    def _():
        pl.semaphore_signal(barrier, inc=1, device_id=z_up, device_id_type=MESH)

    @pl.when(has_down)
    def _():
        pl.semaphore_signal(barrier, inc=1, device_id=z_down, device_id_type=MESH)

    loads[0].wait()
    pl.semaphore_wait(barrier, 4 + has_up.astype(jnp.int32) + has_down.astype(jnp.int32))

    scale = jnp.exp(jnp.full((1, 1), temp_ref[0], F32))
    offset = bias_ref[0]

    theirs = pl.ds(pl.multiple_of(HALF * (1 - f), HALF), HALF)
    mine = pl.ds(pl.multiple_of(HALF * f, HALF), HALF)

    def rows_of(b):
        return pl.ds(pl.multiple_of(b * HALF, HALF), HALF)

    def block(ref, e, b):
        return ref.at[e, rows_of(b)]

    own_t = rows_of(zz)
    send(text.at[theirs], block(tbuf, f, zz), tf_swap.at[0], tf_r.at[zz, f], near_a)

    def t_forward(dist, e, src=None):
        for sign, can, to, sems in ((-1, has_up, z_up, tf_up), (1, has_down, z_down, tf_down)):
            b = zz + sign * dist
            here = (b >= 0) if sign < 0 else (b < LINE)

            @pl.when(here)
            def _():
                if dist > 0:
                    arrived(block(tbuf, e, b), tf_r.at[b, e])

                @pl.when(can)
                def _():
                    origin = block(tbuf, e, b) if src is None else src
                    remote(origin, block(tbuf, e, b), sems.at[dist, e], tf_r.at[b, e], to).start()

    def t_forward_sent(dist, e):
        for sign, can, to, sems in ((-1, has_up, z_up, tf_up), (1, has_down, z_down, tf_down)):
            b = zz + sign * dist
            here = (b >= 0) if sign < 0 else (b < LINE)

            @pl.when(jnp.logical_and(here, can))
            def _():
                remote(block(tbuf, e, b), block(tbuf, e, b), sems.at[dist, e], tf_r.at[b, e], to).wait_send()

    def units(core_at, b):
        return tunit.at[:, pl.ds(pl.multiple_of((core_at * LINE + b) * HALF, HALF), HALF)]

    def normalise(b):
        at = rows_of(b)
        t0 = tbuf[0, at].astype(F32)
        t1 = tbuf[1, at].astype(F32)
        norm = jnp.sqrt(jnp.sum(t0 * t0 + t1 * t1, axis=1, keepdims=True) + EPS)
        tnorms[at] = jnp.broadcast_to(norm, (HALF, 128))
        to = pl.ds(pl.multiple_of((c * LINE + b) * HALF, HALF), HALF)
        tunit[0, to] = (t0 / norm).astype(BF16)
        tunit[1, to] = (t1 / norm).astype(BF16)
        remote(units(c, b), units(c, b), ts_s.at[b], ts_r.at[b], core).start()

    def normalise_at(dist):
        for b, here in ((zz - dist, zz - dist >= 0), (zz + dist, zz + dist < LINE)):

            @pl.when(here)
            def _():
                normalise(b)

    t_forward(0, f, text.at[mine])
    tbuf[f, own_t] = text[mine, :]

    loads[1].wait()
    emb = None
    for cut in range(CUTS):
        loads[2 + cut].wait()
        at = pl.ds(cut * depth, depth)
        term = dot_nn(feats[:, at], proj[at, :])
        emb = term if emb is None else emb + term
    emb_ref[...] = emb

    def img(width, core_at, high, part=None):
        start = (core_at * 2 + high) * ROWS + (0 if part is None else part * HALF)
        size = ROWS if part is None else HALF
        return ibuf.at[width, pl.ds(pl.multiple_of(start, HALF), size)]

    def inorm_of(core_at, high):
        at = pl.ds(pl.multiple_of((core_at * 2 + high) * ROWS, ROWS), ROWS)
        x0 = ibuf[0, at].astype(F32)
        x1 = ibuf[1, at].astype(F32)
        norm = jnp.sqrt(jnp.sum(x0 * x0 + x1 * x1, axis=1, keepdims=True) + EPS)
        inorms[at] = jnp.broadcast_to(norm, (ROWS, 128))

    ibuf[f, pl.ds(pl.multiple_of((c * 2 + h) * ROWS, ROWS), ROWS)] = emb.astype(BF16)

    def give(part_ref, slot, to):
        send(part_ref, part_ref, ig_s.at[slot], ig_r.at[slot], to)

    give(img(f, c, h, 0), 0, near_a)
    give(img(f, c, h, 1), 3, near_b)
    give(img(f, c, h, 1), 1, near_a)
    give(img(f, c, h, 0), 2, near_b)

    def share(piece, slot):
        send(piece, piece, core_s.at[slot], core_r.at[slot], core)

    share(img(f, c, h), 0)
    arrived(block(tbuf, 1 - f, zz), tf_r.at[zz, 1 - f])
    t_forward(0, 1 - f)
    normalise(zz)
    t_forward(1, f)
    t_forward(1, 1 - f)
    normalise_at(1)
    arrived(img(1 - f, c, h, 0), ig_r.at[0])
    give(img(1 - f, c, h, 0), 4, near_b)
    arrived(img(1 - f, c, 1 - h, 1), ig_r.at[3])
    give(img(1 - f, c, 1 - h, 1), 5, near_a)
    arrived(img(1 - f, c, h, 1), ig_r.at[1])
    share(img(1 - f, c, h), 1)
    inorm_of(c, h)
    arrived(img(1 - f, c, 1 - h, 0), ig_r.at[2])
    share(img(1 - f, c, 1 - h), 2)
    t_forward(2, f)
    t_forward(2, 1 - f)
    normalise_at(2)
    arrived(img(f, c, 1 - h, 0), ig_r.at[4])
    arrived(img(f, c, 1 - h, 1), ig_r.at[5])
    share(img(f, c, 1 - h), 3)
    inorm_of(c, 1 - h)
    arrived(img(f, 1 - c, h), core_r.at[0])
    arrived(img(1 - f, 1 - c, h), core_r.at[1])
    inorm_of(1 - c, h)
    arrived(img(1 - f, 1 - c, 1 - h), core_r.at[2])
    arrived(img(f, 1 - c, 1 - h), core_r.at[3])
    inorm_of(1 - c, 1 - h)
    t_forward(3, f)
    t_forward(3, 1 - f)
    normalise_at(3)

    text_rows = LINE * HALF
    t_own = pl.ds(pl.multiple_of(c * text_rows, text_rows), text_rows)
    t_other = pl.ds(pl.multiple_of((1 - c) * text_rows, text_rows), text_rows)
    i_own = pl.ds(pl.multiple_of(c * 2 * ROWS, 2 * ROWS), 2 * ROWS)
    inverse = 1.0 / inorms[...][:, 0:1]
    cosines = (dot_nt(ibuf[0], tunit[0, t_own]) + dot_nt(ibuf[1], tunit[1, t_own])) * inverse
    logits = scale * cosines + offset
    row = lax.broadcasted_iota(jnp.int32, logits.shape, 0) - ((c * 2 + h) * ROWS + HALF * f)
    col = lax.broadcasted_iota(jnp.int32, logits.shape, 1) - zz * HALF
    same = jnp.logical_and(row == col, jnp.logical_and(col >= 0, col < HALF))
    weights = jax.nn.sigmoid(logits) - jnp.where(same, 1.0, 0.0)
    weights_t = jnp.transpose(weights * inverse).astype(BF16)
    weigh[0] = weights
    weigh[1] = weights * cosines

    for e in range(2):
        tacc[e] = dot_nn(weights_t, ibuf[e])

    def t_back(dist):
        for e in range(2):
            for sign, can, to, inbox, r in (
                (-1, has_up, z_down, tright, tb_right),
                (1, has_down, z_up, tleft, tb_left),
            ):
                b = zz + sign * dist
                here = (b >= 0) if sign < 0 else (b < LINE)

                @pl.when(here)
                def _():
                    at = rows_of(b)

                    @pl.when(can)
                    def _():
                        arrived(inbox.at[e, at], r.at[b, e])
                        tsend[e, at] = (tacc[e, at] + inbox[e, at].astype(F32)).astype(BF16)

                    @pl.when(jnp.logical_not(can))
                    def _():
                        tsend[e, at] = tacc[e, at].astype(BF16)

                    remote(tsend.at[e, at], inbox.at[e, at], tb_s.at[b, e], r.at[b, e], to).start()

    def t_back_sent(dist):
        for sign, to, inbox, r in ((-1, z_down, tright, tb_right), (1, z_up, tleft, tb_left)):
            b = zz + sign * dist
            here = (b >= 0) if sign < 0 else (b < LINE)

            @pl.when(here)
            def _():
                at = rows_of(b)
                for e in range(2):
                    remote(tsend.at[e, at], inbox.at[e, at], tb_s.at[b, e], r.at[b, e], to).wait_send()

    t_back(3)

    for b in range(LINE):
        arrived(units(1 - c, b), ts_r.at[b])
    inverse = 1.0 / inorms[i_own][:, 0:1]
    cosines = (dot_nt(ibuf[0, i_own], tunit[0, t_other]) + dot_nt(ibuf[1, i_own], tunit[1, t_other])) * inverse
    weights = jax.nn.sigmoid(scale * cosines + offset)
    wimg[:, t_own] = weigh[0, i_own].astype(BF16)
    wimg[:, t_other] = weights.astype(BF16)

    def mid(high, part=None):
        start = high * ROWS + (0 if part is None else part * HALF)
        return pl.ds(pl.multiple_of(start, HALF), ROWS if part is None else HALF)

    def hand(slot, value, to):
        rsend[slot] = value.astype(BF16)
        send(rsend.at[slot], rrecv.at[slot], rs_s.at[slot], rs_r.at[slot], to)

    value = dot_nn(wimg[mid(1 - h), :], tunit[f])
    hand(4, value[0:HALF], near_a)
    hand(5, value[HALF:], near_b)
    to_b = dot_nn(wimg[mid(1 - h), :], tunit[1 - f])
    hand(3, to_b[HALF:], near_b)
    to_a = dot_nn(wimg[mid(h), :], tunit[1 - f])
    hand(0, to_a[0:HALF], near_a)
    qa[...] = to_a[HALF:]
    qb[...] = to_b[0:HALF]

    products = as_row(jnp.sum(weigh[1, i_own] + weights * cosines, axis=1, keepdims=True))
    dot_out[3, :, 0 : 2 * ROWS] = products
    for slot, high, to in ((0, h, near_a), (1, 1 - h, near_b), (2, 1 - h, far)):
        dot_out[slot, :, 0:ROWS] = dot_out[3, :, pl.ds(pl.multiple_of(high * ROWS, ROWS), ROWS)]
        at = dot_out.at[slot, :, pl.ds(0, ROWS)]
        send(at, dot_in.at[slot], dot_s.at[slot], dot_r.at[slot], to)
    qown[...] = dot_nn(wimg[mid(h), :], tunit[f])

    t_back(2)
    arrived(rrecv.at[4], rs_r.at[4])
    hand(2, qb[...] + rrecv[4].astype(F32), near_b)
    arrived(rrecv.at[5], rs_r.at[5])
    hand(1, qa[...] + rrecv[5].astype(F32), near_a)
    t_back(1)

    for slot in range(3):
        arrived(dot_in.at[slot], dot_r.at[slot])
    idot_row = dot_out[3, 0:1, pl.ds(pl.multiple_of(h * ROWS, ROWS), ROWS)]
    idot = as_column(idot_row + dot_in[0, 0:1, :] + dot_in[1, 0:1, :] + dot_in[2, 0:1, :])
    width = proj.shape[1]
    theirs_h = pl.ds(pl.multiple_of((1 - f) * width, width), width)
    mine_h = pl.ds(pl.multiple_of(f * width, width), width)
    inorm = inorms[pl.ds(pl.multiple_of((c * 2 + h) * ROWS, ROWS), ROWS)][:, 0:1]
    directions = []
    for part in range(2):
        at = pl.ds(part * HALF, HALF)
        for slot in (part, 2 + part):
            arrived(rrecv.at[slot], rs_r.at[slot])
        back = qown[at] + (rrecv[part].astype(F32) + rrecv[2 + part].astype(F32))
        norm = inorm[part * HALF : part * HALF + HALF]
        unit = emb_ref[at] / norm
        direction = ((back - unit * idot[part * HALF : part * HALF + HALF]) * (scale / norm)).astype(BF16)
        ipart[at] = dot_nt(direction, proj[theirs_h, :]).astype(BF16)
        send(ipart.at[at], ipart_in.at[at], ip_s.at[part], ip_r.at[part], near_a)
        directions.append(direction)
    igrad_ref[...] = dot_nt(jnp.concatenate(directions, axis=0), proj[mine_h, :])

    for e in range(2):

        @pl.when(has_down)
        def _():
            arrived(block(tleft, e, zz), tb_left.at[zz, e])
            tacc[e, own_t] = tacc[e, own_t] + tleft[e, own_t].astype(F32)

        @pl.when(has_up)
        def _():
            arrived(block(tright, e, zz), tb_right.at[zz, e])
            tacc[e, own_t] = tacc[e, own_t] + tright[e, own_t].astype(F32)

    tnorm = tnorms[own_t][:, 0:1]
    u0 = tbuf[0, own_t].astype(F32) / tnorm
    u1 = tbuf[1, own_t].astype(F32) / tnorm
    b0 = tacc[0, own_t]
    b1 = tacc[1, own_t]
    tdot = jnp.sum(u0 * b0 + u1 * b1, axis=1, keepdims=True)
    factor = scale / tnorm
    tacc[0, own_t] = (b0 - u0 * tdot) * factor
    tacc[1, own_t] = (b1 - u1 * tdot) * factor
    tpart[...] = tacc[1 - f, own_t].astype(BF16)
    send(tpart, tpart_in, tp_s.at[0], tp_r.at[0], near_a)
    tgrad_ref[mine, :] = tacc[f, own_t]

    for part in range(2):
        at = pl.ds(part * HALF, HALF)
        arrived(ipart_in.at[at], ip_r.at[part])
        igrad_ref[at, :] = igrad_ref[at, :] + ipart_in[at].astype(F32)
    arrived(tpart_in, tp_r.at[0])
    tgrad_ref[theirs, :] = tpart_in[...].astype(F32)

    for copy in sent:
        copy.wait_send()
    for b in range(LINE):
        remote(units(c, b), units(c, b), ts_s.at[b], ts_r.at[b], core).wait_send()
    for dist in range(LINE):
        for e in range(2):
            t_forward_sent(dist, e)
        if dist > 0:
            t_back_sent(dist)


def local(image_feats, text_emb, image_proj, log_temp, bias):
    rows, wide = image_feats.shape
    width = text_emb.shape[1]
    dma = pltpu.SemaphoreType.DMA
    group = 4 * rows
    text_rows = LINE * HALF
    return pl.pallas_call(
        kernel,
        out_shape=(pltpu.VMEM((rows, width), F32), pltpu.VMEM((rows, width), F32)),
        in_specs=[pl.BlockSpec(memory_space=pltpu.HBM)] * 3 + [pl.BlockSpec(memory_space=pltpu.SMEM)] * 2,
        out_specs=(pl.BlockSpec(memory_space=pltpu.VMEM), pl.BlockSpec(memory_space=pltpu.VMEM)),
        scratch_shapes=[
            pltpu.VMEM((rows, wide), BF16),
            pltpu.VMEM((rows, width), BF16),
            pltpu.VMEM((wide, width), BF16),
            pltpu.VMEM((rows, width), F32),
            pltpu.VMEM((2, group, width), BF16),
            pltpu.VMEM((group, 128), F32),
            pltpu.VMEM((2, text_rows, width), BF16),
            pltpu.VMEM((2, 2 * text_rows, width), BF16),
            pltpu.VMEM((text_rows, 128), F32),
            pltpu.VMEM((2, group, text_rows), F32),
            pltpu.VMEM((2 * rows, 2 * text_rows), BF16),
            pltpu.VMEM((2, text_rows, width), F32),
            pltpu.VMEM((2, text_rows, width), BF16),
            pltpu.VMEM((2, text_rows, width), BF16),
            pltpu.VMEM((2, text_rows, width), BF16),
            pltpu.VMEM((rows, width), F32),
            pltpu.VMEM((HALF, width), F32),
            pltpu.VMEM((HALF, width), F32),
            pltpu.VMEM((6, HALF, width), BF16),
            pltpu.VMEM((6, HALF, width), BF16),
            pltpu.VMEM((4, 8, 2 * rows), F32),
            pltpu.VMEM((3, 8, rows), F32),
            pltpu.VMEM((rows, width), BF16),
            pltpu.VMEM((rows, width), BF16),
            pltpu.VMEM((HALF, width), BF16),
            pltpu.VMEM((HALF, width), BF16),
            dma((2 + CUTS,)),
            dma((6,)), dma((6,)),
            dma((4,)), dma((4,)),
            dma((1,)), dma((4, 2)), dma((4, 2)), dma((4, 2)),
            dma((4,)), dma((4,)),
            dma((4, 2)), dma((4, 2)), dma((4, 2)),
            dma((6,)), dma((6,)),
            dma((3,)), dma((3,)),
            dma((2,)), dma((2,)),
            dma((1,)), dma((1,)),
        ],
        compiler_params=pltpu.CompilerParams(
            collective_id=0, has_side_effects=True, vmem_limit_bytes=48 << 20
        ),
        name="contrastive_backward",
    )(*[pltpu.with_memory_space_constraint(x, pltpu.HBM) for x in (image_feats, text_emb, image_proj)], log_temp, bias)


def solution(mesh):
    placed = (P("dp", None), P("dp", "feat"), P(None, "feat"), P(), P())
    return jax.shard_map(
        local,
        mesh=mesh,
        in_specs=placed,
        out_specs=(P("dp", "feat"), P("dp", "feat")),
        check_vma=False,
    )
```

```python
import functools

import jax
import jax.numpy as jnp
from jax import lax
from jax.experimental import pallas as pl
from jax.experimental.pallas import tpu as pltpu
from jax.sharding import PartitionSpec as P

EPS = 1e-06
MESH = pl.DeviceIdType.MESH
F32 = jnp.float32
BF16 = jnp.bfloat16
ROWS = 128
HALF = 64
LINE = 4
CUTS = 4
FORTH = 2
BACK = 1


def dot_nt(left, right):
    return lax.dot_general(left, right, (((1,), (1,)), ((), ())), preferred_element_type=F32)


def dot_nn(left, right):
    return jnp.dot(left, right, preferred_element_type=F32)


def as_row(column):
    n = column.shape[0]
    return jnp.transpose(jnp.broadcast_to(column, (n, 128)))[0:8, :]


def as_column(row):
    n = row.shape[1]
    return jnp.transpose(jnp.broadcast_to(row, (128, n)))[:, 0:1]


def kernel(
    feats_hbm, text_hbm, proj_hbm, temp_ref, bias_ref, igrad_ref, tgrad_ref,
    feats, text, proj, emb_ref, ibuf, inorms, tbuf, tunit, tnorms, weigh, wimg, tacc, tsend, tleft, tright,
    qown, qa, qb, rsend, rrecv, dot_out, dot_in, ipart, ipart_in, tpart, tpart_in,
    lsem, ig_s, ig_r, core_s, core_r, tf_swap, tf_up, tf_down, tf_r, ts_s, ts_r,
    tb_s, tb_left, tb_right, rs_s, rs_r, dot_s, dot_r, ip_s, ip_r, tp_s, tp_r,
):
    dp = lax.axis_index("dp")
    f = lax.axis_index("feat")
    zz = (dp // 4) % 4
    h = (dp // 2) % 2
    c = dp % 2
    opposite = dp + 2 - 4 * h
    core = (dp + 1 - 2 * c, f)
    near_a = (dp, 1 - f)
    near_b = (opposite, 1 - f)
    far = (opposite, f)
    z_up = (dp + 4, f)
    z_down = (dp - 4, f)
    has_up = zz < LINE - 1
    has_down = zz > 0

    def remote(src, dst, send, recv, to):
        return pltpu.make_async_remote_copy(
            src_ref=src, dst_ref=dst, send_sem=send, recv_sem=recv, device_id=to, device_id_type=MESH
        )

    sent = []

    def send(src, dst, s, r, to):
        copy = remote(src, dst, s, r, to)
        copy.start()
        sent.append(copy)
        return copy

    def left(*copies):
        for copy in copies:
            copy.wait_send()
            sent[:] = [other for other in sent if other is not copy]

    def arrived(dst, r):
        remote(dst, dst, tf_swap.at[0], r, core).wait_recv()

    depth = proj.shape[0] // CUTS
    loads = [pltpu.make_async_copy(text_hbm, text, lsem.at[0]), pltpu.make_async_copy(feats_hbm, feats, lsem.at[1])]
    for cut in range(CUTS):
        rows = pl.ds(cut * depth, depth)
        loads.append(pltpu.make_async_copy(proj_hbm.at[rows], proj.at[rows], lsem.at[2 + cut]))
    for load in loads:
        load.start()

    barrier = pltpu.get_barrier_semaphore()
    for peer in (core, near_a, near_b, far):
        pl.semaphore_signal(barrier, inc=1, device_id=peer, device_id_type=MESH)

    @pl.when(has_up)
    def _():
        pl.semaphore_signal(barrier, inc=1, device_id=z_up, device_id_type=MESH)

    @pl.when(has_down)
    def _():
        pl.semaphore_signal(barrier, inc=1, device_id=z_down, device_id_type=MESH)

    loads[0].wait()
    pl.semaphore_wait(barrier, 4 + has_up.astype(jnp.int32) + has_down.astype(jnp.int32))

    scale = jnp.exp(jnp.full((1, 1), temp_ref[0], F32))
    offset = bias_ref[0]

    theirs = pl.ds(pl.multiple_of(HALF * (1 - f), HALF), HALF)
    mine = pl.ds(pl.multiple_of(HALF * f, HALF), HALF)

    def rows_of(b):
        return pl.ds(pl.multiple_of(b * HALF, HALF), HALF)

    def block(ref, e, b, k=0, pieces=1):
        size = HALF // pieces
        return ref.at[e, pl.ds(pl.multiple_of(b * HALF + k * size, size), size)]

    own_t = rows_of(zz)
    for k in range(FORTH):
        piece = text.at[pl.ds(pl.multiple_of(HALF * (1 - f) + k * (HALF // FORTH), HALF // FORTH), HALF // FORTH)]
        send(piece, block(tbuf, f, zz, k, FORTH), tf_swap.at[k], tf_r.at[zz, f * FORTH + k], near_a)

    def t_forward(dist, e, src=False):
        for k in range(FORTH):
            for sign, can, to, sems in ((-1, has_up, z_up, tf_up), (1, has_down, z_down, tf_down)):
                b = zz + sign * dist
                here = (b >= 0) if sign < 0 else (b < LINE)
                sem = e * FORTH + k

                @pl.when(here)
                def _():
                    piece = block(tbuf, e, b, k, FORTH)
                    if dist > 0:
                        arrived(piece, tf_r.at[b, sem])
                    elif not src:
                        if sign < 0:
                            arrived(piece, tf_r.at[b, sem])

                    @pl.when(can)
                    def _():
                        origin = piece
                        if src:
                            size = HALF // FORTH
                            origin = text.at[pl.ds(pl.multiple_of(HALF * f + k * size, size), size)]
                        remote(origin, piece, sems.at[dist, sem], tf_r.at[b, sem], to).start()

    def t_forward_sent(dist, e):
        for k in range(FORTH):
            for sign, can, to, sems in ((-1, has_up, z_up, tf_up), (1, has_down, z_down, tf_down)):
                b = zz + sign * dist
                here = (b >= 0) if sign < 0 else (b < LINE)
                sem = e * FORTH + k

                @pl.when(jnp.logical_and(here, can))
                def _():
                    piece = block(tbuf, e, b, k, FORTH)
                    remote(piece, piece, sems.at[dist, sem], tf_r.at[b, sem], to).wait_send()

    def units(core_at, b):
        return tunit.at[:, pl.ds(pl.multiple_of((core_at * LINE + b) * HALF, HALF), HALF)]

    def normalise(b):
        at = rows_of(b)
        t0 = tbuf[0, at].astype(F32)
        t1 = tbuf[1, at].astype(F32)
        norm = jnp.sqrt(jnp.sum(t0 * t0 + t1 * t1, axis=1, keepdims=True) + EPS)
        tnorms[at] = jnp.broadcast_to(norm, (HALF, 128))
        to = pl.ds(pl.multiple_of((c * LINE + b) * HALF, HALF), HALF)
        tunit[0, to] = (t0 / norm).astype(BF16)
        tunit[1, to] = (t1 / norm).astype(BF16)
        remote(units(c, b), units(c, b), ts_s.at[b], ts_r.at[b], core).start()

    def normalise_at(dist):
        for b, here in ((zz - dist, zz - dist >= 0), (zz + dist, zz + dist < LINE)):

            @pl.when(here)
            def _():
                normalise(b)

    t_forward(0, f, True)
    tbuf[f, own_t] = text[mine, :]

    loads[1].wait()
    emb = None
    for cut in range(CUTS):
        loads[2 + cut].wait()
        at = pl.ds(cut * depth, depth)
        term = dot_nn(feats[:, at], proj[at, :])
        emb = term if emb is None else emb + term
    emb_ref[...] = emb

    def img(width, core_at, high, part=None):
        start = (core_at * 2 + high) * ROWS + (0 if part is None else part * HALF)
        size = ROWS if part is None else HALF
        return ibuf.at[width, pl.ds(pl.multiple_of(start, HALF), size)]

    def inorm_of(core_at, high):
        at = pl.ds(pl.multiple_of((core_at * 2 + high) * ROWS, ROWS), ROWS)
        x0 = ibuf[0, at].astype(F32)
        x1 = ibuf[1, at].astype(F32)
        norm = jnp.sqrt(jnp.sum(x0 * x0 + x1 * x1, axis=1, keepdims=True) + EPS)
        inorms[at] = jnp.broadcast_to(norm, (ROWS, 128))

    ibuf[f, pl.ds(pl.multiple_of((c * 2 + h) * ROWS, ROWS), ROWS)] = emb.astype(BF16)

    def give(part_ref, slot, to):
        return send(part_ref, part_ref, ig_s.at[slot], ig_r.at[slot], to)

    give(img(f, c, h, 0), 0, near_a)
    give(img(f, c, h, 1), 3, near_b)
    give(img(f, c, h, 1), 1, near_a)
    give(img(f, c, h, 0), 2, near_b)

    def share(piece, slot):
        send(piece, piece, core_s.at[slot], core_r.at[slot], core)

    share(img(f, c, h), 0)
    t_forward(0, 1 - f)
    normalise(zz)
    t_forward(1, f)
    t_forward(1, 1 - f)
    normalise_at(1)
    arrived(img(1 - f, c, h, 0), ig_r.at[0])
    give(img(1 - f, c, h, 0), 4, near_b)
    arrived(img(1 - f, c, 1 - h, 1), ig_r.at[3])
    give(img(1 - f, c, 1 - h, 1), 5, near_a)
    arrived(img(1 - f, c, h, 1), ig_r.at[1])
    share(img(1 - f, c, h), 1)
    inorm_of(c, h)
    arrived(img(1 - f, c, 1 - h, 0), ig_r.at[2])
    share(img(1 - f, c, 1 - h), 2)
    t_forward(2, f)
    t_forward(2, 1 - f)
    normalise_at(2)
    arrived(img(f, c, 1 - h, 0), ig_r.at[4])
    arrived(img(f, c, 1 - h, 1), ig_r.at[5])
    share(img(f, c, 1 - h), 3)
    inorm_of(c, 1 - h)
    arrived(img(f, 1 - c, h), core_r.at[0])
    arrived(img(1 - f, 1 - c, h), core_r.at[1])
    inorm_of(1 - c, h)
    arrived(img(1 - f, 1 - c, 1 - h), core_r.at[2])
    arrived(img(f, 1 - c, 1 - h), core_r.at[3])
    inorm_of(1 - c, 1 - h)
    t_forward(3, f)
    t_forward(3, 1 - f)
    normalise_at(3)

    text_rows = LINE * HALF
    t_own = pl.ds(pl.multiple_of(c * text_rows, text_rows), text_rows)
    t_other = pl.ds(pl.multiple_of((1 - c) * text_rows, text_rows), text_rows)
    i_own = pl.ds(pl.multiple_of(c * 2 * ROWS, 2 * ROWS), 2 * ROWS)
    inverse = 1.0 / inorms[...][:, 0:1]
    cosines = (dot_nt(ibuf[0], tunit[0, t_own]) + dot_nt(ibuf[1], tunit[1, t_own])) * inverse
    logits = scale * cosines + offset
    row = lax.broadcasted_iota(jnp.int32, logits.shape, 0) - ((c * 2 + h) * ROWS + HALF * f)
    col = lax.broadcasted_iota(jnp.int32, logits.shape, 1) - zz * HALF
    same = jnp.logical_and(row == col, jnp.logical_and(col >= 0, col < HALF))
    weights = jax.nn.sigmoid(logits) - jnp.where(same, 1.0, 0.0)
    weights_t = jnp.transpose(weights * inverse).astype(BF16)
    weigh[0] = weights
    weigh[1] = weights * cosines

    for e in range(2):
        tacc[e] = dot_nn(weights_t, ibuf[e])

    def t_back(dist):
        for e in range(2):
            for k in range(BACK):
                for sign, can, to, inbox, r in (
                    (-1, has_up, z_down, tright, tb_right),
                    (1, has_down, z_up, tleft, tb_left),
                ):
                    b = zz + sign * dist
                    here = (b >= 0) if sign < 0 else (b < LINE)
                    size = HALF // BACK
                    sem = e * BACK + k

                    @pl.when(here)
                    def _():
                        at = pl.ds(pl.multiple_of(b * HALF + k * size, size), size)

                        @pl.when(can)
                        def _():
                            arrived(inbox.at[e, at], r.at[b, sem])
                            tsend[e, at] = (tacc[e, at] + inbox[e, at].astype(F32)).astype(BF16)

                        @pl.when(jnp.logical_not(can))
                        def _():
                            tsend[e, at] = tacc[e, at].astype(BF16)

                        remote(tsend.at[e, at], inbox.at[e, at], tb_s.at[b, sem], r.at[b, sem], to).start()

    def t_back_sent(dist):
        for sign, to, inbox, r in ((-1, z_down, tright, tb_right), (1, z_up, tleft, tb_left)):
            b = zz + sign * dist
            here = (b >= 0) if sign < 0 else (b < LINE)

            @pl.when(here)
            def _():
                for e in range(2):
                    for k in range(BACK):
                        at = block(tsend, e, b, k, BACK)
                        into = block(inbox, e, b, k, BACK)
                        sem = e * BACK + k
                        remote(at, into, tb_s.at[b, sem], r.at[b, sem], to).wait_send()

    t_back(3)

    for b in range(LINE):
        arrived(units(1 - c, b), ts_r.at[b])
    inverse = 1.0 / inorms[i_own][:, 0:1]
    cosines = (dot_nt(ibuf[0, i_own], tunit[0, t_other]) + dot_nt(ibuf[1, i_own], tunit[1, t_other])) * inverse
    weights = jax.nn.sigmoid(scale * cosines + offset)
    wimg[:, t_own] = weigh[0, i_own].astype(BF16)
    wimg[:, t_other] = weights.astype(BF16)

    def mid(high, part=None):
        start = high * ROWS + (0 if part is None else part * HALF)
        return pl.ds(pl.multiple_of(start, HALF), ROWS if part is None else HALF)

    def hand(slot, value, to):
        rsend[slot] = value.astype(BF16)
        return send(rsend.at[slot], rrecv.at[slot], rs_s.at[slot], rs_r.at[slot], to)

    value = dot_nn(wimg[mid(1 - h), :], tunit[f])
    first = (hand(4, value[0:HALF], near_a), hand(5, value[HALF:], near_b))
    to_b = dot_nn(wimg[mid(1 - h), :], tunit[1 - f])
    to_a = dot_nn(wimg[mid(h), :], tunit[1 - f])
    qa[...] = to_a[HALF:]
    qb[...] = to_b[0:HALF]
    qown[...] = dot_nn(wimg[mid(h), :], tunit[f])

    products = as_row(jnp.sum(weigh[1, i_own] + weights * cosines, axis=1, keepdims=True))
    dot_out[3, :, 0 : 2 * ROWS] = products
    for slot, high, to in ((0, h, near_a), (1, 1 - h, near_b), (2, 1 - h, far)):
        dot_out[slot, :, 0:ROWS] = dot_out[3, :, pl.ds(pl.multiple_of(high * ROWS, ROWS), ROWS)]
        at = dot_out.at[slot, :, pl.ds(0, ROWS)]
        send(at, dot_in.at[slot], dot_s.at[slot], dot_r.at[slot], to)
    left(*first)
    hand(3, to_b[HALF:], near_b)
    hand(0, to_a[0:HALF], near_a)

    t_back(2)
    arrived(rrecv.at[4], rs_r.at[4])
    hand(2, qb[...] + rrecv[4].astype(F32), near_b)
    arrived(rrecv.at[5], rs_r.at[5])
    hand(1, qa[...] + rrecv[5].astype(F32), near_a)
    t_back(1)

    for slot in range(3):
        arrived(dot_in.at[slot], dot_r.at[slot])
    idot_row = dot_out[3, 0:1, pl.ds(pl.multiple_of(h * ROWS, ROWS), ROWS)]
    idot = as_column(idot_row + dot_in[0, 0:1, :] + dot_in[1, 0:1, :] + dot_in[2, 0:1, :])
    width = proj.shape[1]
    theirs_h = pl.ds(pl.multiple_of((1 - f) * width, width), width)
    mine_h = pl.ds(pl.multiple_of(f * width, width), width)
    inorm = inorms[pl.ds(pl.multiple_of((c * 2 + h) * ROWS, ROWS), ROWS)][:, 0:1]
    directions = []
    for part in range(2):
        at = pl.ds(part * HALF, HALF)
        for slot in (part, 2 + part):
            arrived(rrecv.at[slot], rs_r.at[slot])
        back = qown[at] + (rrecv[part].astype(F32) + rrecv[2 + part].astype(F32))
        norm = inorm[part * HALF : part * HALF + HALF]
        unit = emb_ref[at] / norm
        direction = ((back - unit * idot[part * HALF : part * HALF + HALF]) * (scale / norm)).astype(BF16)
        ipart[at] = dot_nt(direction, proj[theirs_h, :]).astype(BF16)
        send(ipart.at[at], ipart_in.at[at], ip_s.at[part], ip_r.at[part], near_a)
        directions.append(direction)
    igrad_ref[...] = dot_nt(jnp.concatenate(directions, axis=0), proj[mine_h, :])

    for e in range(2):

        @pl.when(has_down)
        def _():
            for k in range(BACK):
                arrived(block(tleft, e, zz, k, BACK), tb_left.at[zz, e * BACK + k])
            tacc[e, own_t] = tacc[e, own_t] + tleft[e, own_t].astype(F32)

        @pl.when(has_up)
        def _():
            for k in range(BACK):
                arrived(block(tright, e, zz, k, BACK), tb_right.at[zz, e * BACK + k])
            tacc[e, own_t] = tacc[e, own_t] + tright[e, own_t].astype(F32)

    tnorm = tnorms[own_t][:, 0:1]
    u0 = tbuf[0, own_t].astype(F32) / tnorm
    u1 = tbuf[1, own_t].astype(F32) / tnorm
    b0 = tacc[0, own_t]
    b1 = tacc[1, own_t]
    tdot = jnp.sum(u0 * b0 + u1 * b1, axis=1, keepdims=True)
    factor = scale / tnorm
    tacc[0, own_t] = (b0 - u0 * tdot) * factor
    tacc[1, own_t] = (b1 - u1 * tdot) * factor
    tpart[...] = tacc[1 - f, own_t].astype(BF16)
    send(tpart, tpart_in, tp_s.at[0], tp_r.at[0], near_a)
    tgrad_ref[mine, :] = tacc[f, own_t]

    for part in range(2):
        at = pl.ds(part * HALF, HALF)
        arrived(ipart_in.at[at], ip_r.at[part])
        igrad_ref[at, :] = igrad_ref[at, :] + ipart_in[at].astype(F32)
    arrived(tpart_in, tp_r.at[0])
    tgrad_ref[theirs, :] = tpart_in[...].astype(F32)

    for copy in sent:
        copy.wait_send()
    for b in range(LINE):
        remote(units(c, b), units(c, b), ts_s.at[b], ts_r.at[b], core).wait_send()
    for dist in range(LINE):
        for e in range(2):
            t_forward_sent(dist, e)
        if dist > 0:
            t_back_sent(dist)


def store(igrad_vmem, tgrad_vmem, igrad_ref, tgrad_ref, sems):
    copies = [
        pltpu.make_async_copy(igrad_vmem, igrad_ref, sems.at[0]),
        pltpu.make_async_copy(tgrad_vmem, tgrad_ref, sems.at[1]),
    ]
    for copy in copies:
        copy.start()
    for copy in copies:
        copy.wait()


def local(image_feats, text_emb, image_proj, log_temp, bias):
    rows, wide = image_feats.shape
    width = text_emb.shape[1]
    dma = pltpu.SemaphoreType.DMA
    group = 4 * rows
    text_rows = LINE * HALF
    igrad, tgrad = pl.pallas_call(
        kernel,
        out_shape=(pltpu.VMEM((rows, width), F32), pltpu.VMEM((rows, width), F32)),
        in_specs=[pl.BlockSpec(memory_space=pltpu.HBM)] * 3 + [pl.BlockSpec(memory_space=pltpu.SMEM)] * 2,
        out_specs=(pl.BlockSpec(memory_space=pltpu.VMEM), pl.BlockSpec(memory_space=pltpu.VMEM)),
        scratch_shapes=[
            pltpu.VMEM((rows, wide), BF16),
            pltpu.VMEM((rows, width), BF16),
            pltpu.VMEM((wide, width), BF16),
            pltpu.VMEM((rows, width), F32),
            pltpu.VMEM((2, group, width), BF16),
            pltpu.VMEM((group, 128), F32),
            pltpu.VMEM((2, text_rows, width), BF16),
            pltpu.VMEM((2, 2 * text_rows, width), BF16),
            pltpu.VMEM((text_rows, 128), F32),
            pltpu.VMEM((2, group, text_rows), F32),
            pltpu.VMEM((2 * rows, 2 * text_rows), BF16),
            pltpu.VMEM((2, text_rows, width), F32),
            pltpu.VMEM((2, text_rows, width), BF16),
            pltpu.VMEM((2, text_rows, width), BF16),
            pltpu.VMEM((2, text_rows, width), BF16),
            pltpu.VMEM((rows, width), F32),
            pltpu.VMEM((HALF, width), F32),
            pltpu.VMEM((HALF, width), F32),
            pltpu.VMEM((6, HALF, width), BF16),
            pltpu.VMEM((6, HALF, width), BF16),
            pltpu.VMEM((4, 8, 2 * rows), F32),
            pltpu.VMEM((3, 8, rows), F32),
            pltpu.VMEM((rows, width), BF16),
            pltpu.VMEM((rows, width), BF16),
            pltpu.VMEM((HALF, width), BF16),
            pltpu.VMEM((HALF, width), BF16),
            dma((2 + CUTS,)),
            dma((6,)), dma((6,)),
            dma((4,)), dma((4,)),
            dma((FORTH,)), dma((4, 2 * FORTH)), dma((4, 2 * FORTH)), dma((4, 2 * FORTH)),
            dma((4,)), dma((4,)),
            dma((4, 2 * BACK)), dma((4, 2 * BACK)), dma((4, 2 * BACK)),
            dma((6,)), dma((6,)),
            dma((3,)), dma((3,)),
            dma((2,)), dma((2,)),
            dma((1,)), dma((1,)),
        ],
        compiler_params=pltpu.CompilerParams(
            collective_id=0, has_side_effects=True, vmem_limit_bytes=48 << 20
        ),
        name="contrastive_backward",
    )(*[pltpu.with_memory_space_constraint(x, pltpu.HBM) for x in (image_feats, text_emb, image_proj)], log_temp, bias)
    shape = jax.ShapeDtypeStruct((rows, width), F32)
    return pl.pallas_call(
        store,
        out_shape=(shape, shape),
        in_specs=[pl.BlockSpec(memory_space=pl.ANY)] * 2,
        out_specs=(pl.BlockSpec(memory_space=pl.ANY), pl.BlockSpec(memory_space=pl.ANY)),
        scratch_shapes=[dma((2,))],
        compiler_params=pltpu.CompilerParams(vmem_limit_bytes=1 << 20),
        name="store_gradients",
    )(*[pltpu.with_memory_space_constraint(x, pltpu.VMEM) for x in (igrad, tgrad)])


def solution(mesh):
    placed = (P("dp", None), P("dp", "feat"), P(None, "feat"), P(), P())
    return jax.shard_map(
        local,
        mesh=mesh,
        in_specs=placed,
        out_specs=(P("dp", "feat"), P("dp", "feat")),
        check_vma=False,
    )
```

```python
import functools

import jax
import jax.numpy as jnp
from jax import lax
from jax.experimental import pallas as pl
from jax.experimental.pallas import tpu as pltpu
from jax.sharding import PartitionSpec as P

EPS = 1e-06
MESH = pl.DeviceIdType.MESH
F32 = jnp.float32
BF16 = jnp.bfloat16
ROWS = 128
HALF = 64
LINE = 4
CUTS = 2
FORTH = 2
BACK = 1


def dot_nt(left, right):
    return lax.dot_general(left, right, (((1,), (1,)), ((), ())), preferred_element_type=F32)


def dot_nn(left, right):
    return jnp.dot(left, right, preferred_element_type=F32)


def as_row(column):
    n = column.shape[0]
    return jnp.transpose(jnp.broadcast_to(column, (n, 128)))[0:8, :]


def as_column(row):
    n = row.shape[1]
    return jnp.transpose(jnp.broadcast_to(row, (128, n)))[:, 0:1]


def kernel(
    feats_hbm, text_hbm, proj_hbm, temp_ref, bias_ref, igrad_ref, tgrad_ref,
    feats, text, proj, emb_ref, ibuf, inorms, tbuf, tunit, tnorms, weigh, wimg, tacc, tsend, tleft, tright,
    qown, qa, qb, rsend, rrecv, dot_out, dot_in, ipart, ipart_in, tpart, tpart_in,
    lsem, ig_s, ig_r, core_s, core_r, tf_swap, tf_up, tf_down, tf_r, ts_s, ts_r,
    tb_s, tb_left, tb_right, rs_s, rs_r, dot_s, dot_r, ip_s, ip_r, tp_s, tp_r,
):
    dp = lax.axis_index("dp")
    f = lax.axis_index("feat")
    zz = (dp // 4) % 4
    h = (dp // 2) % 2
    c = dp % 2
    opposite = dp + 2 - 4 * h
    core = (dp + 1 - 2 * c, f)
    near_a = (dp, 1 - f)
    near_b = (opposite, 1 - f)
    far = (opposite, f)
    z_up = (dp + 4, f)
    z_down = (dp - 4, f)
    has_up = zz < LINE - 1
    has_down = zz > 0

    def remote(src, dst, send, recv, to):
        return pltpu.make_async_remote_copy(
            src_ref=src, dst_ref=dst, send_sem=send, recv_sem=recv, device_id=to, device_id_type=MESH
        )

    sent = []

    def send(src, dst, s, r, to):
        copy = remote(src, dst, s, r, to)
        copy.start()
        sent.append(copy)
        return copy

    def left(*copies):
        for copy in copies:
            copy.wait_send()
            sent[:] = [other for other in sent if other is not copy]

    def arrived(dst, r):
        remote(dst, dst, tf_swap.at[0], r, core).wait_recv()

    depth = proj.shape[0] // CUTS
    loads = [pltpu.make_async_copy(text_hbm, text, lsem.at[0]), pltpu.make_async_copy(feats_hbm, feats, lsem.at[1])]
    for cut in range(CUTS):
        rows = pl.ds(cut * depth, depth)
        loads.append(pltpu.make_async_copy(proj_hbm.at[rows], proj.at[rows], lsem.at[2 + cut]))
    for load in loads:
        load.start()

    barrier = pltpu.get_barrier_semaphore()
    for peer in (core, near_a, near_b, far):
        pl.semaphore_signal(barrier, inc=1, device_id=peer, device_id_type=MESH)

    @pl.when(has_up)
    def _():
        pl.semaphore_signal(barrier, inc=1, device_id=z_up, device_id_type=MESH)

    @pl.when(has_down)
    def _():
        pl.semaphore_signal(barrier, inc=1, device_id=z_down, device_id_type=MESH)

    loads[0].wait()
    pl.semaphore_wait(barrier, 4 + has_up.astype(jnp.int32) + has_down.astype(jnp.int32))

    scale = jnp.exp(jnp.full((1, 1), temp_ref[0], F32))
    offset = bias_ref[0]

    theirs = pl.ds(pl.multiple_of(HALF * (1 - f), HALF), HALF)
    mine = pl.ds(pl.multiple_of(HALF * f, HALF), HALF)

    def rows_of(b):
        return pl.ds(pl.multiple_of(b * HALF, HALF), HALF)

    def block(ref, e, b, k=0, pieces=1):
        size = HALF // pieces
        return ref.at[e, pl.ds(pl.multiple_of(b * HALF + k * size, size), size)]

    own_t = rows_of(zz)
    for k in range(FORTH):
        piece = text.at[pl.ds(pl.multiple_of(HALF * (1 - f) + k * (HALF // FORTH), HALF // FORTH), HALF // FORTH)]
        send(piece, block(tbuf, f, zz, k, FORTH), tf_swap.at[k], tf_r.at[zz, f * FORTH + k], near_a)

    def t_forward(dist, e, src=False):
        for k in range(FORTH):
            for sign, can, to, sems in ((-1, has_up, z_up, tf_up), (1, has_down, z_down, tf_down)):
                b = zz + sign * dist
                here = (b >= 0) if sign < 0 else (b < LINE)
                sem = e * FORTH + k

                @pl.when(here)
                def _():
                    piece = block(tbuf, e, b, k, FORTH)
                    if dist > 0:
                        arrived(piece, tf_r.at[b, sem])
                    elif not src:
                        if sign < 0:
                            arrived(piece, tf_r.at[b, sem])

                    @pl.when(can)
                    def _():
                        origin = piece
                        if src:
                            size = HALF // FORTH
                            origin = text.at[pl.ds(pl.multiple_of(HALF * f + k * size, size), size)]
                        remote(origin, piece, sems.at[dist, sem], tf_r.at[b, sem], to).start()

    def t_forward_sent(dist, e):
        for k in range(FORTH):
            for sign, can, to, sems in ((-1, has_up, z_up, tf_up), (1, has_down, z_down, tf_down)):
                b = zz + sign * dist
                here = (b >= 0) if sign < 0 else (b < LINE)
                sem = e * FORTH + k

                @pl.when(jnp.logical_and(here, can))
                def _():
                    piece = block(tbuf, e, b, k, FORTH)
                    remote(piece, piece, sems.at[dist, sem], tf_r.at[b, sem], to).wait_send()

    def units(core_at, b):
        return tunit.at[:, pl.ds(pl.multiple_of((core_at * LINE + b) * HALF, HALF), HALF)]

    def normalise(b):
        at = rows_of(b)
        t0 = tbuf[0, at].astype(F32)
        t1 = tbuf[1, at].astype(F32)
        norm = jnp.sqrt(jnp.sum(t0 * t0 + t1 * t1, axis=1, keepdims=True) + EPS)
        tnorms[at] = jnp.broadcast_to(norm, (HALF, 128))
        to = pl.ds(pl.multiple_of((c * LINE + b) * HALF, HALF), HALF)
        tunit[0, to] = (t0 / norm).astype(BF16)
        tunit[1, to] = (t1 / norm).astype(BF16)
        remote(units(c, b), units(c, b), ts_s.at[b], ts_r.at[b], core).start()

    def normalise_at(dist):
        for b, here in ((zz - dist, zz - dist >= 0), (zz + dist, zz + dist < LINE)):

            @pl.when(here)
            def _():
                normalise(b)

    t_forward(0, f, True)
    tbuf[f, own_t] = text[mine, :]

    loads[1].wait()
    emb = None
    for cut in range(CUTS):
        loads[2 + cut].wait()
        at = pl.ds(cut * depth, depth)
        term = dot_nn(feats[:, at], proj[at, :])
        emb = term if emb is None else emb + term
    emb_ref[...] = emb

    def img(width, core_at, high, part=None):
        start = (core_at * 2 + high) * ROWS + (0 if part is None else part * HALF)
        size = ROWS if part is None else HALF
        return ibuf.at[width, pl.ds(pl.multiple_of(start, HALF), size)]

    def inorm_of(core_at, high):
        at = pl.ds(pl.multiple_of((core_at * 2 + high) * ROWS, ROWS), ROWS)
        x0 = ibuf[0, at].astype(F32)
        x1 = ibuf[1, at].astype(F32)
        norm = jnp.sqrt(jnp.sum(x0 * x0 + x1 * x1, axis=1, keepdims=True) + EPS)
        inorms[at] = jnp.broadcast_to(norm, (ROWS, 128))

    ibuf[f, pl.ds(pl.multiple_of((c * 2 + h) * ROWS, ROWS), ROWS)] = emb.astype(BF16)

    def give(part_ref, slot, to):
        return send(part_ref, part_ref, ig_s.at[slot], ig_r.at[slot], to)

    give(img(f, c, h, 0), 0, near_a)
    give(img(f, c, h, 1), 3, near_b)
    give(img(f, c, h, 1), 1, near_a)
    give(img(f, c, h, 0), 2, near_b)

    def share(piece, slot):
        send(piece, piece, core_s.at[slot], core_r.at[slot], core)

    share(img(f, c, h), 0)
    t_forward(0, 1 - f)
    normalise(zz)
    t_forward(1, f)
    t_forward(1, 1 - f)
    normalise_at(1)
    arrived(img(1 - f, c, h, 0), ig_r.at[0])
    give(img(1 - f, c, h, 0), 4, near_b)
    arrived(img(1 - f, c, 1 - h, 1), ig_r.at[3])
    give(img(1 - f, c, 1 - h, 1), 5, near_a)
    arrived(img(1 - f, c, h, 1), ig_r.at[1])
    share(img(1 - f, c, h), 1)
    inorm_of(c, h)
    arrived(img(1 - f, c, 1 - h, 0), ig_r.at[2])
    share(img(1 - f, c, 1 - h), 2)
    t_forward(2, f)
    t_forward(2, 1 - f)
    normalise_at(2)
    arrived(img(f, c, 1 - h, 0), ig_r.at[4])
    arrived(img(f, c, 1 - h, 1), ig_r.at[5])
    share(img(f, c, 1 - h), 3)
    inorm_of(c, 1 - h)
    arrived(img(f, 1 - c, h), core_r.at[0])
    arrived(img(1 - f, 1 - c, h), core_r.at[1])
    inorm_of(1 - c, h)
    arrived(img(1 - f, 1 - c, 1 - h), core_r.at[2])
    arrived(img(f, 1 - c, 1 - h), core_r.at[3])
    inorm_of(1 - c, 1 - h)
    t_forward(3, f)
    t_forward(3, 1 - f)
    normalise_at(3)

    text_rows = LINE * HALF
    t_own = pl.ds(pl.multiple_of(c * text_rows, text_rows), text_rows)
    t_other = pl.ds(pl.multiple_of((1 - c) * text_rows, text_rows), text_rows)
    i_own = pl.ds(pl.multiple_of(c * 2 * ROWS, 2 * ROWS), 2 * ROWS)
    inverse = 1.0 / inorms[...][:, 0:1]
    cosines = (dot_nt(ibuf[0], tunit[0, t_own]) + dot_nt(ibuf[1], tunit[1, t_own])) * inverse
    logits = scale * cosines + offset
    row = lax.broadcasted_iota(jnp.int32, logits.shape, 0) - ((c * 2 + h) * ROWS + HALF * f)
    col = lax.broadcasted_iota(jnp.int32, logits.shape, 1) - zz * HALF
    same = jnp.logical_and(row == col, jnp.logical_and(col >= 0, col < HALF))
    weights = jax.nn.sigmoid(logits) - jnp.where(same, 1.0, 0.0)
    weights_t = jnp.transpose(weights * inverse).astype(BF16)
    weigh[0] = weights
    weigh[1] = weights * cosines


    def t_back(dist, halves=(0, 1)):
        for e in halves:
            for k in range(BACK):
                for sign, can, to, inbox, r in (
                    (-1, has_up, z_down, tright, tb_right),
                    (1, has_down, z_up, tleft, tb_left),
                ):
                    b = zz + sign * dist
                    here = (b >= 0) if sign < 0 else (b < LINE)
                    size = HALF // BACK
                    sem = e * BACK + k

                    @pl.when(here)
                    def _():
                        at = pl.ds(pl.multiple_of(b * HALF + k * size, size), size)

                        @pl.when(can)
                        def _():
                            arrived(inbox.at[e, at], r.at[b, sem])
                            tsend[e, at] = (tacc[e, at] + inbox[e, at].astype(F32)).astype(BF16)

                        @pl.when(jnp.logical_not(can))
                        def _():
                            tsend[e, at] = tacc[e, at].astype(BF16)

                        remote(tsend.at[e, at], inbox.at[e, at], tb_s.at[b, sem], r.at[b, sem], to).start()

    def t_back_sent(dist):
        for sign, to, inbox, r in ((-1, z_down, tright, tb_right), (1, z_up, tleft, tb_left)):
            b = zz + sign * dist
            here = (b >= 0) if sign < 0 else (b < LINE)

            @pl.when(here)
            def _():
                for e in range(2):
                    for k in range(BACK):
                        at = block(tsend, e, b, k, BACK)
                        into = block(inbox, e, b, k, BACK)
                        sem = e * BACK + k
                        remote(at, into, tb_s.at[b, sem], r.at[b, sem], to).wait_send()

    tacc[0] = dot_nn(weights_t, ibuf[0])
    t_back(3, (0,))

    for b in range(LINE):
        arrived(units(1 - c, b), ts_r.at[b])
    inverse = 1.0 / inorms[i_own][:, 0:1]
    cosines = (dot_nt(ibuf[0, i_own], tunit[0, t_other]) + dot_nt(ibuf[1, i_own], tunit[1, t_other])) * inverse
    weights = jax.nn.sigmoid(scale * cosines + offset)
    wimg[:, t_own] = weigh[0, i_own].astype(BF16)
    wimg[:, t_other] = weights.astype(BF16)

    def mid(high, part=None):
        start = high * ROWS + (0 if part is None else part * HALF)
        return pl.ds(pl.multiple_of(start, HALF), ROWS if part is None else HALF)

    def hand(slot, value, to):
        rsend[slot] = value.astype(BF16)
        return send(rsend.at[slot], rrecv.at[slot], rs_s.at[slot], rs_r.at[slot], to)

    value = dot_nn(wimg[mid(1 - h), :], tunit[f])
    first = (hand(4, value[0:HALF], near_a), hand(5, value[HALF:], near_b))
    tacc[1] = dot_nn(weights_t, ibuf[1])
    t_back(3, (1,))
    to_b = dot_nn(wimg[mid(1 - h), :], tunit[1 - f])
    to_a = dot_nn(wimg[mid(h), :], tunit[1 - f])
    qa[...] = to_a[HALF:]
    qb[...] = to_b[0:HALF]
    qown[...] = dot_nn(wimg[mid(h), :], tunit[f])

    products = as_row(jnp.sum(weigh[1, i_own] + weights * cosines, axis=1, keepdims=True))
    dot_out[3, :, 0 : 2 * ROWS] = products
    for slot, high, to in ((0, h, near_a), (1, 1 - h, near_b), (2, 1 - h, far)):
        dot_out[slot, :, 0:ROWS] = dot_out[3, :, pl.ds(pl.multiple_of(high * ROWS, ROWS), ROWS)]
        at = dot_out.at[slot, :, pl.ds(0, ROWS)]
        send(at, dot_in.at[slot], dot_s.at[slot], dot_r.at[slot], to)
    left(*first)
    hand(3, to_b[HALF:], near_b)
    hand(0, to_a[0:HALF], near_a)

    t_back(2)
    arrived(rrecv.at[4], rs_r.at[4])
    hand(2, qb[...] + rrecv[4].astype(F32), near_b)
    arrived(rrecv.at[5], rs_r.at[5])
    hand(1, qa[...] + rrecv[5].astype(F32), near_a)
    t_back(1)

    for slot in range(3):
        arrived(dot_in.at[slot], dot_r.at[slot])
    idot_row = dot_out[3, 0:1, pl.ds(pl.multiple_of(h * ROWS, ROWS), ROWS)]
    idot = as_column(idot_row + dot_in[0, 0:1, :] + dot_in[1, 0:1, :] + dot_in[2, 0:1, :])
    width = proj.shape[1]
    theirs_h = pl.ds(pl.multiple_of((1 - f) * width, width), width)
    mine_h = pl.ds(pl.multiple_of(f * width, width), width)
    inorm = inorms[pl.ds(pl.multiple_of((c * 2 + h) * ROWS, ROWS), ROWS)][:, 0:1]
    directions = []
    for part in range(2):
        at = pl.ds(part * HALF, HALF)
        for slot in (part, 2 + part):
            arrived(rrecv.at[slot], rs_r.at[slot])
        back = qown[at] + (rrecv[part].astype(F32) + rrecv[2 + part].astype(F32))
        norm = inorm[part * HALF : part * HALF + HALF]
        unit = emb_ref[at] / norm
        direction = ((back - unit * idot[part * HALF : part * HALF + HALF]) * (scale / norm)).astype(BF16)
        ipart[at] = dot_nt(direction, proj[theirs_h, :]).astype(BF16)
        send(ipart.at[at], ipart_in.at[at], ip_s.at[part], ip_r.at[part], near_a)
        directions.append(direction)

    for e in range(2):

        @pl.when(has_down)
        def _():
            for k in range(BACK):
                arrived(block(tleft, e, zz, k, BACK), tb_left.at[zz, e * BACK + k])
            tacc[e, own_t] = tacc[e, own_t] + tleft[e, own_t].astype(F32)

        @pl.when(has_up)
        def _():
            for k in range(BACK):
                arrived(block(tright, e, zz, k, BACK), tb_right.at[zz, e * BACK + k])
            tacc[e, own_t] = tacc[e, own_t] + tright[e, own_t].astype(F32)

    for part in range(2):
        size = HALF // 2
        at = pl.ds(pl.multiple_of(zz * HALF + part * size, size), size)
        norm = tnorms[at][:, 0:1]
        u0 = tbuf[0, at].astype(F32) / norm
        u1 = tbuf[1, at].astype(F32) / norm
        b0 = tacc[0, at]
        b1 = tacc[1, at]
        tdot = jnp.sum(u0 * b0 + u1 * b1, axis=1, keepdims=True)
        factor = scale / norm
        tacc[0, at] = (b0 - u0 * tdot) * factor
        tacc[1, at] = (b1 - u1 * tdot) * factor
        to = pl.ds(part * size, size)
        tpart[to] = tacc[1 - f, at].astype(BF16)
        send(tpart.at[to], tpart_in.at[to], tp_s.at[part], tp_r.at[part], near_a)
    tgrad_ref[mine, :] = tacc[f, own_t]
    igrad_ref[...] = dot_nt(jnp.concatenate(directions, axis=0), proj[mine_h, :])

    for part in range(2):
        at = pl.ds(part * HALF, HALF)
        arrived(ipart_in.at[at], ip_r.at[part])
        igrad_ref[at, :] = igrad_ref[at, :] + ipart_in[at].astype(F32)
    for part in range(2):
        arrived(tpart_in.at[pl.ds(part * (HALF // 2), HALF // 2)], tp_r.at[part])
    tgrad_ref[theirs, :] = tpart_in[...].astype(F32)

    for copy in sent:
        copy.wait_send()
    for b in range(LINE):
        remote(units(c, b), units(c, b), ts_s.at[b], ts_r.at[b], core).wait_send()
    for dist in range(LINE):
        for e in range(2):
            t_forward_sent(dist, e)
        if dist > 0:
            t_back_sent(dist)


def store(igrad_vmem, tgrad_vmem, igrad_ref, tgrad_ref, sems):
    copies = [
        pltpu.make_async_copy(igrad_vmem, igrad_ref, sems.at[0]),
        pltpu.make_async_copy(tgrad_vmem, tgrad_ref, sems.at[1]),
    ]
    for copy in copies:
        copy.start()
    for copy in copies:
        copy.wait()


def local(image_feats, text_emb, image_proj, log_temp, bias):
    rows, wide = image_feats.shape
    width = text_emb.shape[1]
    dma = pltpu.SemaphoreType.DMA
    group = 4 * rows
    text_rows = LINE * HALF
    igrad, tgrad = pl.pallas_call(
        kernel,
        out_shape=(pltpu.VMEM((rows, width), F32), pltpu.VMEM((rows, width), F32)),
        in_specs=[pl.BlockSpec(memory_space=pltpu.HBM)] * 3 + [pl.BlockSpec(memory_space=pltpu.SMEM)] * 2,
        out_specs=(pl.BlockSpec(memory_space=pltpu.VMEM), pl.BlockSpec(memory_space=pltpu.VMEM)),
        scratch_shapes=[
            pltpu.VMEM((rows, wide), BF16),
            pltpu.VMEM((rows, width), BF16),
            pltpu.VMEM((wide, width), BF16),
            pltpu.VMEM((rows, width), F32),
            pltpu.VMEM((2, group, width), BF16),
            pltpu.VMEM((group, 128), F32),
            pltpu.VMEM((2, text_rows, width), BF16),
            pltpu.VMEM((2, 2 * text_rows, width), BF16),
            pltpu.VMEM((text_rows, 128), F32),
            pltpu.VMEM((2, group, text_rows), F32),
            pltpu.VMEM((2 * rows, 2 * text_rows), BF16),
            pltpu.VMEM((2, text_rows, width), F32),
            pltpu.VMEM((2, text_rows, width), BF16),
            pltpu.VMEM((2, text_rows, width), BF16),
            pltpu.VMEM((2, text_rows, width), BF16),
            pltpu.VMEM((rows, width), F32),
            pltpu.VMEM((HALF, width), F32),
            pltpu.VMEM((HALF, width), F32),
            pltpu.VMEM((6, HALF, width), BF16),
            pltpu.VMEM((6, HALF, width), BF16),
            pltpu.VMEM((4, 8, 2 * rows), F32),
            pltpu.VMEM((3, 8, rows), F32),
            pltpu.VMEM((rows, width), BF16),
            pltpu.VMEM((rows, width), BF16),
            pltpu.VMEM((HALF, width), BF16),
            pltpu.VMEM((HALF, width), BF16),
            dma((2 + CUTS,)),
            dma((6,)), dma((6,)),
            dma((4,)), dma((4,)),
            dma((FORTH,)), dma((4, 2 * FORTH)), dma((4, 2 * FORTH)), dma((4, 2 * FORTH)),
            dma((4,)), dma((4,)),
            dma((4, 2 * BACK)), dma((4, 2 * BACK)), dma((4, 2 * BACK)),
            dma((6,)), dma((6,)),
            dma((3,)), dma((3,)),
            dma((2,)), dma((2,)),
            dma((2,)), dma((2,)),
        ],
        compiler_params=pltpu.CompilerParams(
            collective_id=0, has_side_effects=True, vmem_limit_bytes=48 << 20
        ),
        name="contrastive_backward",
    )(*[pltpu.with_memory_space_constraint(x, pltpu.HBM) for x in (image_feats, text_emb, image_proj)], log_temp, bias)
    shape = jax.ShapeDtypeStruct((rows, width), F32)
    return pl.pallas_call(
        store,
        out_shape=(shape, shape),
        in_specs=[pl.BlockSpec(memory_space=pl.ANY)] * 2,
        out_specs=(pl.BlockSpec(memory_space=pl.ANY), pl.BlockSpec(memory_space=pl.ANY)),
        scratch_shapes=[dma((2,))],
        compiler_params=pltpu.CompilerParams(vmem_limit_bytes=1 << 20),
        name="store_gradients",
    )(*[pltpu.with_memory_space_constraint(x, pltpu.VMEM) for x in (igrad, tgrad)])


def solution(mesh):
    placed = (P("dp", None), P("dp", "feat"), P(None, "feat"), P(), P())
    return jax.shard_map(
        local,
        mesh=mesh,
        in_specs=placed,
        out_specs=(P("dp", "feat"), P("dp", "feat")),
        check_vma=False,
    )
```

```python
import functools

import jax
import jax.numpy as jnp
from jax import lax
from jax.experimental import pallas as pl
from jax.experimental.pallas import tpu as pltpu
from jax.sharding import PartitionSpec as P

EPS = 1e-06
MESH = pl.DeviceIdType.MESH
F32 = jnp.float32
BF16 = jnp.bfloat16
ROWS = 128
HALF = 64
LONG = 96
LINE = 4
CUTS = 2
FORTH = 2
BACK = 1


def dot_nt(left, right):
    return lax.dot_general(left, right, (((1,), (1,)), ((), ())), preferred_element_type=F32)


def dot_nn(left, right):
    return jnp.dot(left, right, preferred_element_type=F32)


def as_row(column):
    n = column.shape[0]
    return jnp.transpose(jnp.broadcast_to(column, (n, 128)))[0:8, :]


def as_column(row):
    n = row.shape[1]
    return jnp.transpose(jnp.broadcast_to(row, (128, n)))[:, 0:1]


def kernel(
    feats_hbm, text_hbm, proj_hbm, temp_ref, bias_ref, igrad_ref, tgrad_ref,
    feats, text, proj, emb_ref, ibuf, inorms, tbuf, tunit, tnorms, weigh, wimg, tacc, tsend, tleft, tright,
    qown, qa, qb, rsend, rrecv, dot_out, dot_in, ipart, ipart_in, tpart, tpart_in,
    lsem, ig_s, ig_r, core_s, core_r, tf_swap, tf_up, tf_down, tf_r, ts_s, ts_r,
    tb_s, tb_left, tb_right, rs_s, rs_r, dot_s, dot_r, ip_s, ip_r, tp_s, tp_r,
):
    dp = lax.axis_index("dp")
    f = lax.axis_index("feat")
    zz = (dp // 4) % 4
    h = (dp // 2) % 2
    c = dp % 2
    opposite = dp + 2 - 4 * h
    core = (dp + 1 - 2 * c, f)
    near_a = (dp, 1 - f)
    near_b = (opposite, 1 - f)
    far = (opposite, f)
    z_up = (dp + 4, f)
    z_down = (dp - 4, f)
    has_up = zz < LINE - 1
    has_down = zz > 0

    def remote(src, dst, send, recv, to):
        return pltpu.make_async_remote_copy(
            src_ref=src, dst_ref=dst, send_sem=send, recv_sem=recv, device_id=to, device_id_type=MESH
        )

    sent = []

    def send(src, dst, s, r, to):
        copy = remote(src, dst, s, r, to)
        copy.start()
        sent.append(copy)
        return copy

    def left(*copies):
        for copy in copies:
            copy.wait_send()
            sent[:] = [other for other in sent if other is not copy]

    def arrived(dst, r):
        remote(dst, dst, tf_swap.at[0], r, core).wait_recv()

    depth = proj.shape[0] // CUTS
    loads = [pltpu.make_async_copy(text_hbm, text, lsem.at[0]), pltpu.make_async_copy(feats_hbm, feats, lsem.at[1])]
    for cut in range(CUTS):
        rows = pl.ds(cut * depth, depth)
        loads.append(pltpu.make_async_copy(proj_hbm.at[rows], proj.at[rows], lsem.at[2 + cut]))
    for load in loads:
        load.start()

    barrier = pltpu.get_barrier_semaphore()
    for peer in (core, near_a, near_b, far):
        pl.semaphore_signal(barrier, inc=1, device_id=peer, device_id_type=MESH)

    @pl.when(has_up)
    def _():
        pl.semaphore_signal(barrier, inc=1, device_id=z_up, device_id_type=MESH)

    @pl.when(has_down)
    def _():
        pl.semaphore_signal(barrier, inc=1, device_id=z_down, device_id_type=MESH)

    loads[0].wait()
    pl.semaphore_wait(barrier, 4 + has_up.astype(jnp.int32) + has_down.astype(jnp.int32))

    scale = jnp.exp(jnp.full((1, 1), temp_ref[0], F32))
    offset = bias_ref[0]

    theirs = pl.ds(pl.multiple_of(HALF * (1 - f), HALF), HALF)
    mine = pl.ds(pl.multiple_of(HALF * f, HALF), HALF)

    def rows_of(b):
        return pl.ds(pl.multiple_of(b * HALF, HALF), HALF)

    def block(ref, e, b, k=0, pieces=1):
        size = HALF // pieces
        return ref.at[e, pl.ds(pl.multiple_of(b * HALF + k * size, size), size)]

    own_t = rows_of(zz)
    for k in range(FORTH):
        piece = text.at[pl.ds(pl.multiple_of(HALF * (1 - f) + k * (HALF // FORTH), HALF // FORTH), HALF // FORTH)]
        send(piece, block(tbuf, f, zz, k, FORTH), tf_swap.at[k], tf_r.at[zz, f * FORTH + k], near_a)

    def t_forward(dist, e, src=False):
        for k in range(FORTH):
            for sign, can, to, sems in ((-1, has_up, z_up, tf_up), (1, has_down, z_down, tf_down)):
                b = zz + sign * dist
                here = (b >= 0) if sign < 0 else (b < LINE)
                sem = e * FORTH + k

                @pl.when(here)
                def _():
                    piece = block(tbuf, e, b, k, FORTH)
                    if dist > 0:
                        arrived(piece, tf_r.at[b, sem])
                    elif not src:
                        if sign < 0:
                            arrived(piece, tf_r.at[b, sem])

                    @pl.when(can)
                    def _():
                        origin = piece
                        if src:
                            size = HALF // FORTH
                            origin = text.at[pl.ds(pl.multiple_of(HALF * f + k * size, size), size)]
                        remote(origin, piece, sems.at[dist, sem], tf_r.at[b, sem], to).start()

    def t_forward_sent(dist, e):
        for k in range(FORTH):
            for sign, can, to, sems in ((-1, has_up, z_up, tf_up), (1, has_down, z_down, tf_down)):
                b = zz + sign * dist
                here = (b >= 0) if sign < 0 else (b < LINE)
                sem = e * FORTH + k

                @pl.when(jnp.logical_and(here, can))
                def _():
                    piece = block(tbuf, e, b, k, FORTH)
                    remote(piece, piece, sems.at[dist, sem], tf_r.at[b, sem], to).wait_send()

    def units(core_at, b):
        return tunit.at[:, pl.ds(pl.multiple_of((core_at * LINE + b) * HALF, HALF), HALF)]

    def normalise(b):
        at = rows_of(b)
        t0 = tbuf[0, at].astype(F32)
        t1 = tbuf[1, at].astype(F32)
        norm = jnp.sqrt(jnp.sum(t0 * t0 + t1 * t1, axis=1, keepdims=True) + EPS)
        tnorms[at] = jnp.broadcast_to(norm, (HALF, 128))
        to = pl.ds(pl.multiple_of((c * LINE + b) * HALF, HALF), HALF)
        tunit[0, to] = (t0 / norm).astype(BF16)
        tunit[1, to] = (t1 / norm).astype(BF16)
        remote(units(c, b), units(c, b), ts_s.at[b], ts_r.at[b], core).start()

    def normalise_at(dist):
        for b, here in ((zz - dist, zz - dist >= 0), (zz + dist, zz + dist < LINE)):

            @pl.when(here)
            def _():
                normalise(b)

    t_forward(0, f, True)
    tbuf[f, own_t] = text[mine, :]

    loads[1].wait()
    emb = None
    for cut in range(CUTS):
        loads[2 + cut].wait()
        at = pl.ds(cut * depth, depth)
        term = dot_nn(feats[:, at], proj[at, :])
        emb = term if emb is None else emb + term
    emb_ref[...] = emb

    def img(width, core_at, high, part=None):
        start = (core_at * 2 + high) * ROWS + (0 if part is None else part * LONG)
        size = ROWS if part is None else (LONG, ROWS - LONG)[part]
        return ibuf.at[width, pl.ds(pl.multiple_of(start, ROWS - LONG), size)]

    def inorm_of(core_at, high):
        at = pl.ds(pl.multiple_of((core_at * 2 + high) * ROWS, ROWS), ROWS)
        x0 = ibuf[0, at].astype(F32)
        x1 = ibuf[1, at].astype(F32)
        norm = jnp.sqrt(jnp.sum(x0 * x0 + x1 * x1, axis=1, keepdims=True) + EPS)
        inorms[at] = jnp.broadcast_to(norm, (ROWS, 128))

    ibuf[f, pl.ds(pl.multiple_of((c * 2 + h) * ROWS, ROWS), ROWS)] = emb.astype(BF16)

    def give(part_ref, slot, to):
        return send(part_ref, part_ref, ig_s.at[slot], ig_r.at[slot], to)

    give(img(f, c, h, 0), 0, near_a)
    give(img(f, c, h, 1), 3, near_b)
    give(img(f, c, h, 1), 1, near_a)
    give(img(f, c, h, 0), 2, near_b)

    def share(piece, slot):
        send(piece, piece, core_s.at[slot], core_r.at[slot], core)

    share(img(f, c, h), 0)
    t_forward(0, 1 - f)
    normalise(zz)
    t_forward(1, f)
    t_forward(1, 1 - f)
    normalise_at(1)
    arrived(img(1 - f, c, h, 0), ig_r.at[0])
    give(img(1 - f, c, h, 0), 4, near_b)
    arrived(img(1 - f, c, 1 - h, 1), ig_r.at[3])
    give(img(1 - f, c, 1 - h, 1), 5, near_a)
    arrived(img(1 - f, c, h, 1), ig_r.at[1])
    share(img(1 - f, c, h), 1)
    inorm_of(c, h)
    arrived(img(1 - f, c, 1 - h, 0), ig_r.at[2])
    share(img(1 - f, c, 1 - h), 2)
    t_forward(2, f)
    t_forward(2, 1 - f)
    normalise_at(2)
    arrived(img(f, c, 1 - h, 0), ig_r.at[4])
    arrived(img(f, c, 1 - h, 1), ig_r.at[5])
    share(img(f, c, 1 - h), 3)
    inorm_of(c, 1 - h)
    arrived(img(f, 1 - c, h), core_r.at[0])
    arrived(img(1 - f, 1 - c, h), core_r.at[1])
    inorm_of(1 - c, h)
    arrived(img(1 - f, 1 - c, 1 - h), core_r.at[2])
    arrived(img(f, 1 - c, 1 - h), core_r.at[3])
    inorm_of(1 - c, 1 - h)
    t_forward(3, f)
    t_forward(3, 1 - f)
    normalise_at(3)

    text_rows = LINE * HALF
    t_own = pl.ds(pl.multiple_of(c * text_rows, text_rows), text_rows)
    t_other = pl.ds(pl.multiple_of((1 - c) * text_rows, text_rows), text_rows)
    i_own = pl.ds(pl.multiple_of(c * 2 * ROWS, 2 * ROWS), 2 * ROWS)
    inverse = 1.0 / inorms[...][:, 0:1]
    cosines = (dot_nt(ibuf[0], tunit[0, t_own]) + dot_nt(ibuf[1], tunit[1, t_own])) * inverse
    logits = scale * cosines + offset
    row = lax.broadcasted_iota(jnp.int32, logits.shape, 0) - ((c * 2 + h) * ROWS + HALF * f)
    col = lax.broadcasted_iota(jnp.int32, logits.shape, 1) - zz * HALF
    same = jnp.logical_and(row == col, jnp.logical_and(col >= 0, col < HALF))
    weights = jax.nn.sigmoid(logits) - jnp.where(same, 1.0, 0.0)
    weights_t = jnp.transpose(weights * inverse).astype(BF16)
    weigh[0] = weights
    weigh[1] = weights * cosines


    def t_back(dist, halves=(0, 1)):
        for e in halves:
            for k in range(BACK):
                for sign, can, to, inbox, r in (
                    (-1, has_up, z_down, tright, tb_right),
                    (1, has_down, z_up, tleft, tb_left),
                ):
                    b = zz + sign * dist
                    here = (b >= 0) if sign < 0 else (b < LINE)
                    size = HALF // BACK
                    sem = e * BACK + k

                    @pl.when(here)
                    def _():
                        at = pl.ds(pl.multiple_of(b * HALF + k * size, size), size)

                        @pl.when(can)
                        def _():
                            arrived(inbox.at[e, at], r.at[b, sem])
                            tsend[e, at] = (tacc[e, at] + inbox[e, at].astype(F32)).astype(BF16)

                        @pl.when(jnp.logical_not(can))
                        def _():
                            tsend[e, at] = tacc[e, at].astype(BF16)

                        remote(tsend.at[e, at], inbox.at[e, at], tb_s.at[b, sem], r.at[b, sem], to).start()

    def t_back_sent(dist):
        for sign, to, inbox, r in ((-1, z_down, tright, tb_right), (1, z_up, tleft, tb_left)):
            b = zz + sign * dist
            here = (b >= 0) if sign < 0 else (b < LINE)

            @pl.when(here)
            def _():
                for e in range(2):
                    for k in range(BACK):
                        at = block(tsend, e, b, k, BACK)
                        into = block(inbox, e, b, k, BACK)
                        sem = e * BACK + k
                        remote(at, into, tb_s.at[b, sem], r.at[b, sem], to).wait_send()

    tacc[0] = dot_nn(weights_t, ibuf[0])
    t_back(3, (0,))

    for b in range(LINE):
        arrived(units(1 - c, b), ts_r.at[b])
    inverse = 1.0 / inorms[i_own][:, 0:1]
    cosines = (dot_nt(ibuf[0, i_own], tunit[0, t_other]) + dot_nt(ibuf[1, i_own], tunit[1, t_other])) * inverse
    weights = jax.nn.sigmoid(scale * cosines + offset)
    wimg[:, t_own] = weigh[0, i_own].astype(BF16)
    wimg[:, t_other] = weights.astype(BF16)

    def mid(high, part=None):
        start = high * ROWS + (0 if part is None else part * HALF)
        return pl.ds(pl.multiple_of(start, HALF), ROWS if part is None else HALF)

    def hand(slot, value, to):
        rsend[slot] = value.astype(BF16)
        return send(rsend.at[slot], rrecv.at[slot], rs_s.at[slot], rs_r.at[slot], to)

    value = dot_nn(wimg[mid(1 - h), :], tunit[f])
    first = (hand(4, value[0:HALF], near_a), hand(5, value[HALF:], near_b))
    tacc[1] = dot_nn(weights_t, ibuf[1])
    t_back(3, (1,))
    to_b = dot_nn(wimg[mid(1 - h), :], tunit[1 - f])
    to_a = dot_nn(wimg[mid(h), :], tunit[1 - f])
    qa[...] = to_a[HALF:]
    qb[...] = to_b[0:HALF]
    qown[...] = dot_nn(wimg[mid(h), :], tunit[f])

    products = as_row(jnp.sum(weigh[1, i_own] + weights * cosines, axis=1, keepdims=True))
    dot_out[3, :, 0 : 2 * ROWS] = products
    for slot, high, to in ((0, h, near_a), (1, 1 - h, near_b), (2, 1 - h, far)):
        dot_out[slot, :, 0:ROWS] = dot_out[3, :, pl.ds(pl.multiple_of(high * ROWS, ROWS), ROWS)]
        at = dot_out.at[slot, :, pl.ds(0, ROWS)]
        send(at, dot_in.at[slot], dot_s.at[slot], dot_r.at[slot], to)
    left(*first)
    hand(3, to_b[HALF:], near_b)
    hand(0, to_a[0:HALF], near_a)

    t_back(2)
    arrived(rrecv.at[4], rs_r.at[4])
    hand(2, qb[...] + rrecv[4].astype(F32), near_b)
    arrived(rrecv.at[5], rs_r.at[5])
    hand(1, qa[...] + rrecv[5].astype(F32), near_a)
    t_back(1)

    for slot in range(3):
        arrived(dot_in.at[slot], dot_r.at[slot])
    idot_row = dot_out[3, 0:1, pl.ds(pl.multiple_of(h * ROWS, ROWS), ROWS)]
    idot = as_column(idot_row + dot_in[0, 0:1, :] + dot_in[1, 0:1, :] + dot_in[2, 0:1, :])
    width = proj.shape[1]
    theirs_h = pl.ds(pl.multiple_of((1 - f) * width, width), width)
    mine_h = pl.ds(pl.multiple_of(f * width, width), width)
    inorm = inorms[pl.ds(pl.multiple_of((c * 2 + h) * ROWS, ROWS), ROWS)][:, 0:1]
    directions = []
    for part in range(2):
        at = pl.ds(part * HALF, HALF)
        for slot in (part, 2 + part):
            arrived(rrecv.at[slot], rs_r.at[slot])
        back = qown[at] + (rrecv[part].astype(F32) + rrecv[2 + part].astype(F32))
        norm = inorm[part * HALF : part * HALF + HALF]
        unit = emb_ref[at] / norm
        direction = ((back - unit * idot[part * HALF : part * HALF + HALF]) * (scale / norm)).astype(BF16)
        ipart[at] = dot_nt(direction, proj[theirs_h, :]).astype(BF16)
        send(ipart.at[at], ipart_in.at[at], ip_s.at[part], ip_r.at[part], near_a)
        directions.append(direction)

    for e in range(2):

        @pl.when(has_down)
        def _():
            for k in range(BACK):
                arrived(block(tleft, e, zz, k, BACK), tb_left.at[zz, e * BACK + k])
            tacc[e, own_t] = tacc[e, own_t] + tleft[e, own_t].astype(F32)

        @pl.when(has_up)
        def _():
            for k in range(BACK):
                arrived(block(tright, e, zz, k, BACK), tb_right.at[zz, e * BACK + k])
            tacc[e, own_t] = tacc[e, own_t] + tright[e, own_t].astype(F32)

    for part in range(2):
        size = HALF // 2
        at = pl.ds(pl.multiple_of(zz * HALF + part * size, size), size)
        norm = tnorms[at][:, 0:1]
        u0 = tbuf[0, at].astype(F32) / norm
        u1 = tbuf[1, at].astype(F32) / norm
        b0 = tacc[0, at]
        b1 = tacc[1, at]
        tdot = jnp.sum(u0 * b0 + u1 * b1, axis=1, keepdims=True)
        factor = scale / norm
        tacc[0, at] = (b0 - u0 * tdot) * factor
        tacc[1, at] = (b1 - u1 * tdot) * factor
        to = pl.ds(part * size, size)
        tpart[to] = tacc[1 - f, at].astype(BF16)
        send(tpart.at[to], tpart_in.at[to], tp_s.at[part], tp_r.at[part], near_a)
    tgrad_ref[mine, :] = tacc[f, own_t]
    igrad_ref[...] = dot_nt(jnp.concatenate(directions, axis=0), proj[mine_h, :])

    for part in range(2):
        at = pl.ds(part * HALF, HALF)
        arrived(ipart_in.at[at], ip_r.at[part])
        igrad_ref[at, :] = igrad_ref[at, :] + ipart_in[at].astype(F32)
    for part in range(2):
        arrived(tpart_in.at[pl.ds(part * (HALF // 2), HALF // 2)], tp_r.at[part])
    tgrad_ref[theirs, :] = tpart_in[...].astype(F32)

    for copy in sent:
        copy.wait_send()
    for b in range(LINE):
        remote(units(c, b), units(c, b), ts_s.at[b], ts_r.at[b], core).wait_send()
    for dist in range(LINE):
        for e in range(2):
            t_forward_sent(dist, e)
        if dist > 0:
            t_back_sent(dist)


def store(igrad_vmem, tgrad_vmem, igrad_ref, tgrad_ref, sems):
    copies = [
        pltpu.make_async_copy(igrad_vmem, igrad_ref, sems.at[0]),
        pltpu.make_async_copy(tgrad_vmem, tgrad_ref, sems.at[1]),
    ]
    for copy in copies:
        copy.start()
    for copy in copies:
        copy.wait()


def local(image_feats, text_emb, image_proj, log_temp, bias):
    rows, wide = image_feats.shape
    width = text_emb.shape[1]
    dma = pltpu.SemaphoreType.DMA
    group = 4 * rows
    text_rows = LINE * HALF
    igrad, tgrad = pl.pallas_call(
        kernel,
        out_shape=(pltpu.VMEM((rows, width), F32), pltpu.VMEM((rows, width), F32)),
        in_specs=[pl.BlockSpec(memory_space=pltpu.HBM)] * 3 + [pl.BlockSpec(memory_space=pltpu.SMEM)] * 2,
        out_specs=(pl.BlockSpec(memory_space=pltpu.VMEM), pl.BlockSpec(memory_space=pltpu.VMEM)),
        scratch_shapes=[
            pltpu.VMEM((rows, wide), BF16),
            pltpu.VMEM((rows, width), BF16),
            pltpu.VMEM((wide, width), BF16),
            pltpu.VMEM((rows, width), F32),
            pltpu.VMEM((2, group, width), BF16),
            pltpu.VMEM((group, 128), F32),
            pltpu.VMEM((2, text_rows, width), BF16),
            pltpu.VMEM((2, 2 * text_rows, width), BF16),
            pltpu.VMEM((text_rows, 128), F32),
            pltpu.VMEM((2, group, text_rows), F32),
            pltpu.VMEM((2 * rows, 2 * text_rows), BF16),
            pltpu.VMEM((2, text_rows, width), F32),
            pltpu.VMEM((2, text_rows, width), BF16),
            pltpu.VMEM((2, text_rows, width), BF16),
            pltpu.VMEM((2, text_rows, width), BF16),
            pltpu.VMEM((rows, width), F32),
            pltpu.VMEM((HALF, width), F32),
            pltpu.VMEM((HALF, width), F32),
            pltpu.VMEM((6, HALF, width), BF16),
            pltpu.VMEM((6, HALF, width), BF16),
            pltpu.VMEM((4, 8, 2 * rows), F32),
            pltpu.VMEM((3, 8, rows), F32),
            pltpu.VMEM((rows, width), BF16),
            pltpu.VMEM((rows, width), BF16),
            pltpu.VMEM((HALF, width), BF16),
            pltpu.VMEM((HALF, width), BF16),
            dma((2 + CUTS,)),
            dma((6,)), dma((6,)),
            dma((4,)), dma((4,)),
            dma((FORTH,)), dma((4, 2 * FORTH)), dma((4, 2 * FORTH)), dma((4, 2 * FORTH)),
            dma((4,)), dma((4,)),
            dma((4, 2 * BACK)), dma((4, 2 * BACK)), dma((4, 2 * BACK)),
            dma((6,)), dma((6,)),
            dma((3,)), dma((3,)),
            dma((2,)), dma((2,)),
            dma((2,)), dma((2,)),
        ],
        compiler_params=pltpu.CompilerParams(
            collective_id=0, has_side_effects=True, vmem_limit_bytes=48 << 20
        ),
        name="contrastive_backward",
    )(*[pltpu.with_memory_space_constraint(x, pltpu.HBM) for x in (image_feats, text_emb, image_proj)], log_temp, bias)
    shape = jax.ShapeDtypeStruct((rows, width), F32)
    return pl.pallas_call(
        store,
        out_shape=(shape, shape),
        in_specs=[pl.BlockSpec(memory_space=pl.ANY)] * 2,
        out_specs=(pl.BlockSpec(memory_space=pl.ANY), pl.BlockSpec(memory_space=pl.ANY)),
        scratch_shapes=[dma((2,))],
        compiler_params=pltpu.CompilerParams(vmem_limit_bytes=1 << 20),
        name="store_gradients",
    )(*[pltpu.with_memory_space_constraint(x, pltpu.VMEM) for x in (igrad, tgrad)])


def solution(mesh):
    placed = (P("dp", None), P("dp", "feat"), P(None, "feat"), P(), P())
    return jax.shard_map(
        local,
        mesh=mesh,
        in_specs=placed,
        out_specs=(P("dp", "feat"), P("dp", "feat")),
        check_vma=False,
    )
```
